32 devices in a mesh: req: 16 (over z, x, core), mdl: 2 (over y).
Axes of the slice: x: 2, y: 2, z: 4, core: 2. Of those that a mesh axis runs over, the one named last changes fastest.
Arguments:
- hidden_in: bfloat16 [2048, 2048], P('req'), may hold values from -6 to 6
- z_weight: bfloat16 [2048, 4096], P('req', 'mdl'), may hold values from -0.125 to 0.125
- x_weight: bfloat16 [2048, 4096], P('req', 'mdl'), may hold values from -0.125 to 0.125
- state_proj: bfloat16 [2048, 256], P('req'), may hold values from -0.125 to 0.125
- step_weight: bfloat16 [2048, 64], P('req', 'mdl'), may hold values from -0.125 to 0.125
- step_bias: float32 [64], P('mdl'), may hold values from -4 to -1
- decay_log: float32 [64], P('mdl'), may hold values from -2 to 1
- skip_gain: float32 [64], P('mdl'), may hold values from 0.5 to 2
- conv_inner: float32 [4, 4096], P(None, 'mdl'), may hold values from -3 to 3
- conv_state: float32 [4, 256], replicated, may hold values from -3 to 3
- norm_gain: float32 [4096], P('mdl'), may hold values from 0.1 to 1.9
- out_weight: bfloat16 [4096, 2048], P('mdl', 'req'), may hold values from -0.09375 to 0.09375
- state_pool: float32 [128, 64, 64, 128], P('req', 'mdl'), may hold values from -2.4 to 2.4
- conv_pool_inner: bfloat16 [128, 3, 4096], P('req', None, 'mdl'), may hold values from -6 to 6
- conv_pool_state: bfloat16 [128, 3, 256], P('req'), may hold values from -6 to 6
- owner_dev: int32 [128], replicated, may hold values from 0 to 15, as said below
- state_page: int32 [128], replicated, may hold values from 0 to 7, as said below
- conv_page: int32 [128], replicated, may hold values from 0 to 7, as said below
- accepted: int32 [128], replicated, may hold values from 1 to 16
Outputs:
- mixed: bfloat16 [2048, 2048], P('req', 'mdl')
- new_states: float32 [128, 64, 64, 128], P('req', 'mdl')
- conv_inner_out: bfloat16 [128, 3, 4096], P('req', None, 'mdl')
- conv_state_out: bfloat16 [128, 3, 256], P('req')
The draws below stay inside these ranges and needn't reach their ends.
Inputs may be any that keep to these rules, and one draw needn't show every extreme that they name: `owner_dev`: request r of device i = r // 8 has its owner among devices i to i + 7 along req, counted modulo the axis size; among the 8 requests of one device at most 2 name the same owner, and exactly 2 do for one owner; every owner is named by exactly 8 requests in all. `state_page`: the requests of one owner have distinct state slots. `conv_page`: the requests of one owner have distinct convolution pages.
All inputs are finite; a program needn't handle non-finite values.
Results may differ from the reference program's by a relative error of at most 0.0069.
Values may be sent and summed in bfloat16 or wider, within the bound.
No kernel may reach another device: no remote copies, remote signals or barrier semaphores. Data moves between devices by JAX's collectives and lax.ppermute only.
A program may use at most 128 MiB of HBM per device.

```python
import jax
import jax.numpy as jnp
from jax import lax

D = 2048
HEADS = 64
HDIM = 64
NSTATE = 128
KCONV = 4
DRAFT = 16
CAP = 2
WINDOW = 8
REQ_DEV = 8
INNER = 4096
REQUESTS = 128
TOKENS = 2048


def slot_order(key):
    return jax.random.permutation(key, REQ_DEV).astype(jnp.int32)


def routing(key):
    groups = REQUESTS // REQ_DEV
    keys = jax.random.split(jax.random.fold_in(key, 11), 5)
    distinct = jax.random.permutation(keys[1], WINDOW).astype(jnp.int32)[:REQ_DEV - CAP + 1]
    offsets = jnp.concatenate([jnp.full((CAP - 1,), distinct[0], jnp.int32), distinct])
    offsets = offsets[jax.random.permutation(keys[2], REQ_DEV)]
    homes = jnp.arange(groups, dtype=jnp.int32)[:, None]
    owners = (homes + offsets[None, :]) % groups
    columns = jnp.arange(REQ_DEV, dtype=jnp.int32)[None, :]
    state_perm = jax.vmap(slot_order)(jax.random.split(keys[3], groups))
    conv_perm = jax.vmap(slot_order)(jax.random.split(keys[4], groups))
    state_pages = state_perm[owners, columns]
    conv_pages = conv_perm[owners, columns]
    return (owners.reshape(-1).astype(jnp.int32), state_pages.reshape(-1).astype(jnp.int32), conv_pages.reshape(-1).astype(jnp.int32))


def draw_owner_dev(key, part):
    return routing(key)[0]


def draw_state_page(key, part):
    return routing(key)[1]


def draw_conv_page(key, part):
    return routing(key)[2]


def touch_ends(values, own_key, low, high):
    shape = values.shape
    spot = [jax.random.randint(jax.random.fold_in(own_key, axis), (), 0, shape[axis]) for axis in range(len(shape))]
    values = values.at[tuple(spot)].set(low)
    longest = shape.index(max(shape))
    spot[longest] = (spot[longest] + 1) % shape[longest]
    return values.at[tuple(spot)].set(high)


def block_levels(own_key, shape, pieces, low, largest):
    gain, own = 1.0, jax.random.fold_in(own_key, 6)
    for dim, shards_of in pieces:
        heights = jnp.exp(jax.random.uniform(jax.random.fold_in(own, dim), (shards_of,), jnp.float32, low / len(pieces), largest / len(pieces)))
        gain = gain * jnp.repeat(heights, shape[dim] // shards_of).reshape([-1 if axis == dim else 1 for axis in range(len(shape))])
    return gain


def bell_draw(stream_key, dims, deviation, bound, shards=(), kind=jnp.bfloat16):
    level = block_levels(stream_key, dims, shards, -0.22, 0.18) if shards else 1.0
    result = jax.random.normal(stream_key, dims, jnp.float32) * deviation * level
    return jnp.minimum(jnp.maximum(result, -bound), bound).astype(kind)


def setup_inputs(seed: int = 0) -> dict:
    key_list = jax.random.split(jax.random.key(seed), 20)
    return {
        "hidden_in": bell_draw(key_list[0], (TOKENS, D), 1.0, 6.0, ((0, 16),)),
        "z_weight": bell_draw(key_list[1], (D, INNER), D ** -0.5, 0.125, ((0, 16), (1, 2))),
        "x_weight": bell_draw(key_list[2], (D, INNER), D ** -0.5, 0.125, ((0, 16), (1, 2))),
        "state_proj": bell_draw(key_list[3], (D, 2 * NSTATE), D ** -0.5, 0.125, ((0, 16),)),
        "step_weight": bell_draw(key_list[4], (D, HEADS), D ** -0.5, 0.125, ((0, 16), (1, 2))),
        "step_bias": jnp.clip(-4.0 + 3.0 * jax.random.uniform(key_list[5], (HEADS,), jnp.float32) ** block_levels(key_list[5], (HEADS,), ((0, 2),), -0.2, 0.2), -4.0, -1.0),
        "decay_log": jnp.clip(-2.0 + 3.0 * jax.random.uniform(key_list[6], (HEADS,), jnp.float32) ** block_levels(key_list[6], (HEADS,), ((0, 2),), -0.2, 0.2), -2.0, 1.0),
        "skip_gain": jnp.clip(0.5 + 1.5 * jax.random.uniform(key_list[7], (HEADS,), jnp.float32) ** block_levels(key_list[7], (HEADS,), ((0, 2),), -0.2, 0.2), 0.5, 2.0),
        "conv_inner": bell_draw(key_list[8], (KCONV, INNER), KCONV ** -0.5, 3.0, ((1, 2),), jnp.float32),
        "conv_state": bell_draw(key_list[9], (KCONV, 2 * NSTATE), KCONV ** -0.5, 3.0, (), jnp.float32),
        "norm_gain": jnp.clip(1.0 + 0.18 * jax.random.normal(key_list[10], (INNER,), jnp.float32), 0.1, 1.9),
        "out_weight": bell_draw(key_list[11], (INNER, D), INNER ** -0.5, 0.09375, ((0, 2), (1, 16))),
        "state_pool": bell_draw(key_list[12], (REQUESTS, HEADS, HDIM, NSTATE), 0.3, 2.4, ((0, 16), (1, 2)), jnp.float32),
        "conv_pool_inner": bell_draw(key_list[13], (REQUESTS, KCONV - 1, INNER), 1.0, 6.0, ((0, 16), (2, 2))),
        "conv_pool_state": bell_draw(key_list[14], (REQUESTS, KCONV - 1, 2 * NSTATE), 1.0, 6.0, ((0, 16),)),
        "owner_dev": draw_owner_dev(jax.random.fold_in(key_list[19], 71), 0),
        "state_page": draw_state_page(jax.random.fold_in(key_list[19], 71), 0),
        "conv_page": draw_conv_page(jax.random.fold_in(key_list[19], 71), 0),
        "accepted": touch_ends(jax.random.randint(key_list[18], (REQUESTS,), 1, DRAFT + 1), jax.random.fold_in(key_list[18], 1), 1, DRAFT).astype(jnp.int32),
    }


HIGH = lax.Precision.HIGHEST
EPSILON = 1e-05

def reference(hidden_in, z_weight, x_weight, state_proj, step_weight, step_bias, decay_log, skip_gain, conv_inner, conv_state, norm_gain, out_weight, state_pool, conv_pool_inner, conv_pool_state, owner_dev, state_page, conv_page, accepted):
    gate_pre = jnp.dot(hidden_in, z_weight, preferred_element_type=jnp.float32)
    inner_raw = jnp.dot(hidden_in, x_weight, preferred_element_type=jnp.float32).astype(jnp.bfloat16)
    state_raw = jnp.dot(hidden_in, state_proj, preferred_element_type=jnp.float32).astype(jnp.bfloat16)
    step_raw = jnp.dot(hidden_in, step_weight, preferred_element_type=jnp.float32).astype(jnp.bfloat16)
    packed = jnp.concatenate([inner_raw, state_raw], axis=1).reshape(REQUESTS, DRAFT, INNER + 2 * NSTATE)
    step_rows = step_raw.reshape(REQUESTS, DRAFT, HEADS)
    history = jnp.concatenate([conv_pool_inner, conv_pool_state], axis=2)
    kernel = jnp.concatenate([conv_inner, conv_state], axis=1)
    state_slot = (owner_dev * REQ_DEV + state_page).astype(jnp.int32)
    conv_slot = (owner_dev * REQ_DEV + conv_page).astype(jnp.int32)
    rate = -jnp.exp(decay_log)

    def one_request(item):
        rows, step_in, slot_state, slot_conv, kept_count = item
        series = jnp.concatenate([history[slot_conv], rows], axis=0)
        series_f = series.astype(jnp.float32)
        conv_sum = kernel[0] * series_f[0:DRAFT]
        for tap in range(1, KCONV):
            conv_sum = conv_sum + kernel[tap] * series_f[tap:tap + DRAFT]
        active = jax.nn.silu(conv_sum)
        inputs_x = active[:, :INNER].reshape(DRAFT, HEADS, HDIM)
        b_rows = active[:, INNER:INNER + NSTATE]
        c_rows = active[:, INNER + NSTATE:]
        step_size = jax.nn.softplus(step_in.astype(jnp.float32) + step_bias)
        decay = jnp.exp(step_size * rate)
        start_state = state_pool[slot_state]

        def advance(carry, inputs):
            state_now, chosen = carry
            x_row, b_row, c_row, size_row, decay_row, index_now = inputs
            state_now = decay_row[:, None, None] * state_now + (size_row[:, None] * x_row)[:, :, None] * b_row[None, None, :]
            y_row = jnp.einsum('hpn,n->hp', state_now, c_row, precision=HIGH) + skip_gain[:, None] * x_row
            chosen = jnp.where(index_now + 1 == kept_count, state_now, chosen)
            return ((state_now, chosen), y_row)
        steps_index = jnp.arange(DRAFT, dtype=jnp.int32)
        (final_state, chosen), y_rows = lax.scan(advance, (start_state, jnp.zeros_like(start_state)), (inputs_x, b_rows, c_rows, step_size, decay, steps_index))
        edge_rows = lax.dynamic_slice_in_dim(series, kept_count.astype(jnp.int32), KCONV - 1, 0)
        return (y_rows.reshape(DRAFT, INNER).astype(jnp.bfloat16), chosen, edge_rows)
    mixed_inner, chosen_all, edges_all = lax.map(one_request, (packed, step_rows, state_slot, conv_slot, accepted))
    gated = mixed_inner.reshape(TOKENS, INNER).astype(jnp.float32) * jax.nn.silu(gate_pre)
    mean_square = lax.optimization_barrier(jnp.mean(gated * gated, axis=1, keepdims=True))
    normed = (gated * lax.rsqrt(mean_square + EPSILON) * norm_gain).astype(jnp.bfloat16)
    mixed = jnp.dot(normed, out_weight, preferred_element_type=jnp.float32).astype(jnp.bfloat16)
    new_states = jnp.zeros_like(state_pool).at[state_slot].set(chosen_all)
    conv_out = jnp.zeros_like(history).at[conv_slot].set(edges_all)
    return (mixed, new_states, conv_out[:, :, :INNER], conv_out[:, :, INNER:])
```

```python
import jax
import jax.numpy as jnp
from jax import lax
from jax.experimental import pallas as pl
from jax.experimental.pallas import tpu as pltpu
from jax.sharding import Mesh, PartitionSpec as P

KCONV = 4
CAP = 2
WINDOW = 8
LANES = 128
EPSILON = 1e-05
HIGH = lax.Precision.HIGHEST
BF16 = jnp.bfloat16
F32 = jnp.float32

RING = ("slab", "side", "core")


def round_up(value, unit):
    return -(-value // unit) * unit


def factor(count):
    core = 2 if count % 2 == 0 else 1
    chips = count // core
    side = 1
    while (2 * side) ** 2 <= chips and chips % (2 * side) == 0:
        side *= 2
    return chips // side, side, core


def rotate(value, axis, steps):
    count = lax.axis_size(axis)
    if steps % count == 0:
        return value
    pairs = [(source, (source + steps) % count) for source in range(count)]
    return lax.ppermute(value, axis, pairs)


def gather_axis(value, axis, dim):
    count = lax.axis_size(axis)
    if count == 1:
        return value
    if count > 2:
        return lax.all_gather(value, axis, axis=dim, tiled=True)
    peer = rotate(value, axis, 1)
    first = lax.axis_index(axis) == 0
    return jnp.concatenate(
        [jnp.where(first, value, peer), jnp.where(first, peer, value)], axis=dim
    )


def place(pieces, slots):
    full = jnp.zeros((len(pieces),) + pieces[0].shape, pieces[0].dtype)
    for piece, slot in zip(pieces, slots):
        full = lax.dynamic_update_slice_in_dim(full, piece[None], slot, 0)
    return full


def one_hot_apply(table, values, shape):
    flat = values.reshape(table.shape[1], -1)
    return jnp.dot(table, flat, preferred_element_type=F32).astype(BF16).reshape(shape)


def route_tables(owner_dev, state_page, conv_page, accepted, groups, per_dev, this_dev):
    owner_grid = owner_dev.reshape(groups, per_dev)
    home_grid = jnp.arange(groups, dtype=jnp.int32)[:, None]
    offset_grid = (owner_grid - home_grid + groups) % groups
    positions = jnp.arange(per_dev, dtype=jnp.int32)
    earlier = positions[None, :] < positions[:, None]
    pair_rank = jnp.sum((owner_grid[:, :, None] == owner_grid[:, None, :]) & earlier[None], axis=2)
    slot_grid = offset_grid * CAP + pair_rank
    send_at = lax.dynamic_slice_in_dim(slot_grid, this_dev, 1, 0)[0]
    buffer_rows = jnp.arange(WINDOW * CAP, dtype=jnp.int32)
    send_table = (buffer_rows[:, None] == send_at[None, :]).astype(BF16)
    arrive_at = slot_grid.reshape(-1)
    slot_match = (owner_dev[None, :] == this_dev) & (state_page[None, :] == positions[:, None])
    pick_from = jnp.sum(jnp.where(slot_match, arrive_at[None, :], 0), axis=1)
    conv_of = jnp.sum(jnp.where(slot_match, conv_page[None, :], 0), axis=1)
    kept_count = jnp.sum(jnp.where(slot_match, accepted[None, :], 0), axis=1)
    gather_table = (buffer_rows[None, :] == pick_from[:, None]).astype(BF16)
    return (send_table, gather_table, conv_of, kept_count)


def series_tables(conv_of, kept_count, per_dev, draft, hist_pad):
    rows = per_dev * draft
    keep = KCONV - 1
    row = jnp.arange(rows, dtype=jnp.int32)
    step = row % draft
    page_row = jnp.repeat(conv_of, draft) * keep
    columns = jnp.arange(rows + hist_pad, dtype=jnp.int32)
    shifts = []
    for delay in range(1, KCONV):
        source = jnp.where(step >= delay, row - delay, rows + page_row + keep + step - delay)
        shifts.append((columns[None, :] == source[:, None]).astype(BF16))
    out_row = jnp.arange(hist_pad, dtype=jnp.int32)
    out_page, out_at = out_row // keep, out_row % keep
    match = conv_of[None, :] == out_page[:, None]
    slot_of = jnp.sum(jnp.where(match, jnp.arange(per_dev, dtype=jnp.int32)[None, :], 0), axis=1)
    kept_of = jnp.sum(jnp.where(match, kept_count[None, :], 0), axis=1)
    at = kept_of + out_at
    source = jnp.where(at < keep, rows + out_page * keep + at, slot_of * draft + at - keep)
    edges = (columns[None, :] == source[:, None]).astype(BF16)
    kept_row = jnp.repeat(kept_count, draft)
    before = jnp.broadcast_to((step < kept_row)[:, None], (rows, LANES)).astype(F32)
    end_row = row - step + kept_row - 1
    at_end = (row[None, :] == end_row[:, None]).astype(F32)
    causal = ((row[:, None] // draft == row[None, :] // draft) & (row[None, :] <= row[:, None])).astype(F32)
    return jnp.stack(shifts), edges, before, at_end, causal


def split_pair(value):
    high = value.astype(BF16)
    return high, (value - high.astype(F32)).astype(BF16)


def convolve(series, current, taps, shift_ref):
    total = taps[KCONV - 1 : KCONV] * current
    for delay in range(1, KCONV):
        moved = jnp.dot(shift_ref[delay - 1], series, preferred_element_type=F32)
        total = total + taps[KCONV - 1 - delay : KCONV - delay] * moved
    return total / (1.0 + jnp.exp(-total))


def mixer_kernel(
    sizes,
    order_ref,
    x_ref,
    aux_ref,
    select_ref,
    shift_ref,
    edge_ref,
    before_ref,
    at_end_ref,
    causal_ref,
    hist_ref,
    hist_state_ref,
    taps_ref,
    taps_state_ref,
    skip_ref,
    bias_ref,
    rate_ref,
    state_ref,
    y_ref,
    new_state_ref,
    conv_ref,
    conv_state_ref,
    b_scr,
    c_scr,
    scores_scr,
    log_scr,
    sel_scr,
    end_scr,
    log_t_scr,
    step_t_scr,
):
    chunks, per_dev, draft, heads, head_dim, state_width = sizes
    rows = per_dev * draft
    width = heads * head_dim
    group = pl.program_id(0)
    causal = causal_ref[...]

    @pl.when(group == 0)
    def prepare():
        aux = jnp.dot(aux_ref[0], select_ref[0], preferred_element_type=F32)
        for chunk in range(1, chunks):
            aux = aux + jnp.dot(aux_ref[chunk], select_ref[chunk], preferred_element_type=F32)
        maps = aux[:, : 2 * state_width]
        series = jnp.concatenate([maps.astype(BF16), hist_state_ref[...]], axis=0)
        active = convolve(series, maps, taps_state_ref[...], shift_ref)
        conv_state_ref[...] = jnp.dot(edge_ref[...], series, preferred_element_type=F32).astype(BF16)
        b_rows, c_rows = active[:, :state_width], active[:, state_width:]
        b_scr[...] = b_rows
        c_scr[...] = c_rows
        scores_scr[...] = lax.dot_general(
            c_rows, b_rows, (((1,), (1,)), ((), ())), precision=HIGH, preferred_element_type=F32
        ) * causal
        raw = aux[:, 2 * state_width :] + bias_ref[...]
        step_size = jnp.maximum(raw, 0.0) + jnp.log1p(jnp.exp(-jnp.abs(raw)))
        log_decay = jnp.dot(causal, step_size * rate_ref[...], precision=HIGH, preferred_element_type=F32)
        end = jnp.dot(at_end_ref[...], log_decay, precision=HIGH, preferred_element_type=F32)
        kept = before_ref[...] > 0.0
        chosen = jnp.where(kept, jnp.exp(jnp.where(kept, end - log_decay, 0.0)), 0.0) * step_size
        decay_end = jnp.exp(end)
        for chunk in range(chunks):
            part = slice(chunk * heads, (chunk + 1) * heads)
            log_scr[chunk] = log_decay[:, part]
            sel_scr[chunk] = chosen[:, part]
            end_scr[chunk] = decay_end[:, part]
        log_t_scr[...] = log_decay.T
        step_t_scr[...] = step_size.T

    x_rows = x_ref[0]
    series = jnp.concatenate([x_rows, hist_ref[0]], axis=0)
    active = convolve(series, x_rows.astype(F32), taps_ref[0], shift_ref)
    conv_ref[0] = jnp.dot(edge_ref[...], series, preferred_element_type=F32).astype(BF16)
    scores = scores_scr[...]
    log_here = log_scr[group]
    sel_here = sel_scr[group]
    end_here = end_scr[group]
    within, growth, picks = [], [], []
    for head in range(heads):
        lanes = slice(head * head_dim, (head + 1) * head_dim)
        at = group * heads + head
        log_row = log_t_scr[pl.ds(at, 1), :]
        step_row = step_t_scr[pl.ds(at, 1), :]
        spread = jnp.where(causal > 0.0, log_here[:, head : head + 1] - log_row, -1e30)
        weight = jnp.exp(spread) * (scores * step_row)
        within.append(
            jnp.dot(weight.astype(BF16), active[:, lanes].astype(BF16), preferred_element_type=F32)
        )
        growth.append(jnp.broadcast_to(jnp.exp(log_here[:, head : head + 1]), (rows, head_dim)))
        picks.append(jnp.broadcast_to(sel_here[:, head : head + 1], (rows, head_dim)))
    within = jnp.concatenate(within, axis=1)
    growth = jnp.concatenate(growth, axis=1)
    picked = active[:, :width] * jnp.concatenate(picks, axis=1)
    carried = []
    for slot in range(per_dev):
        part = slice(slot * draft, (slot + 1) * draft)
        state = state_ref[slot].reshape(width, state_width)
        carried.append(
            lax.dot_general(
                c_scr[part, :].astype(BF16),
                state.astype(BF16),
                (((1,), (1,)), ((), ())),
                preferred_element_type=F32,
            )
        )
        x_high, x_low = split_pair(picked[part])
        b_high, b_low = split_pair(b_scr[part, :])
        update = lax.dot_general(
            jnp.concatenate([x_high, x_low, x_high], axis=0),
            jnp.concatenate([b_high, b_high, b_low], axis=0),
            (((0,), (0,)), ((), ())),
            preferred_element_type=F32,
        )
        for head in range(heads):
            keep = end_here[slot * draft : slot * draft + 1, head : head + 1]
            lanes = slice(head * head_dim, (head + 1) * head_dim)
            new_state_ref[slot, head] = keep * state[lanes] + update[lanes]
    carried = jnp.concatenate(carried, axis=0)
    outputs = within + growth * carried + skip_ref[0][:, :width] * active[:, :width]
    if width < y_ref.shape[2]:
        outputs = jnp.concatenate(
            [outputs, jnp.zeros((rows, y_ref.shape[2] - width), F32)], axis=1
        )
    y_ref[0] = outputs.astype(BF16)


def mix_requests(
    packed,
    order,
    select,
    tables,
    history,
    history_state,
    taps,
    taps_state,
    skip_lanes,
    bias,
    rate,
    state_pool,
):
    chunks, rows, packed_width = packed.shape
    per_dev, all_heads, head_dim, state_width = state_pool.shape
    heads = all_heads // chunks
    draft = rows // per_dev
    lanes = history.shape[2]
    aux_lanes = packed_width - lanes
    hist_pad = history.shape[1]
    shifts, edges, before, at_end, causal = tables
    sizes = (chunks, per_dev, draft, heads, head_dim, state_width)

    def whole(array):
        zeros = (0,) * array.ndim
        return pl.BlockSpec(array.shape, lambda group, order_ref: zeros)

    def by_group(block):
        return pl.BlockSpec(
            (1,) + block, lambda group, order_ref: (group,) + (0,) * len(block)
        )

    state_spec = pl.BlockSpec(
        (per_dev, heads, head_dim, state_width), lambda group, order_ref: (0, group, 0, 0)
    )
    step_lanes = select.shape[2] - 2 * state_width
    grid_spec = pltpu.PrefetchScalarGridSpec(
        num_scalar_prefetch=1,
        grid=(chunks,),
        in_specs=[
            pl.BlockSpec((1, rows, lanes), lambda group, order_ref: (order_ref[group], 0, 0)),
            pl.BlockSpec((chunks, rows, aux_lanes), lambda group, order_ref: (0, 0, lanes // aux_lanes)),
            whole(select),
            whole(shifts),
            whole(edges),
            whole(before),
            whole(at_end),
            whole(causal),
            by_group((hist_pad, lanes)),
            whole(history_state),
            by_group((KCONV, lanes)),
            whole(taps_state),
            by_group((1, lanes)),
            whole(bias),
            whole(rate),
            state_spec,
        ],
        out_specs=[
            by_group((rows, lanes)),
            state_spec,
            by_group((hist_pad, lanes)),
            pl.BlockSpec((hist_pad, 2 * state_width), lambda group, order_ref: (0, 0)),
        ],
        scratch_shapes=[
            pltpu.VMEM((rows, state_width), F32),
            pltpu.VMEM((rows, state_width), F32),
            pltpu.VMEM((rows, rows), F32),
            pltpu.VMEM((chunks, rows, heads), F32),
            pltpu.VMEM((chunks, rows, heads), F32),
            pltpu.VMEM((chunks, rows, heads), F32),
            pltpu.VMEM((step_lanes, rows), F32),
            pltpu.VMEM((step_lanes, rows), F32),
        ],
    )
    return pl.pallas_call(
        lambda *refs: mixer_kernel(sizes, *refs),
        grid_spec=grid_spec,
        out_shape=(
            jax.ShapeDtypeStruct((chunks, rows, lanes), BF16),
            jax.ShapeDtypeStruct(state_pool.shape, F32),
            jax.ShapeDtypeStruct((chunks, hist_pad, lanes), BF16),
            jax.ShapeDtypeStruct((hist_pad, 2 * state_width), BF16),
        ),
        compiler_params=pltpu.CompilerParams(vmem_limit_bytes=32 * 1024 * 1024),
        cost_estimate=pl.CostEstimate(
            flops=2 * 4 * rows * rows * all_heads * head_dim,
            bytes_accessed=2 * 4 * state_pool.size,
            transcendentals=rows * rows * all_heads,
        ),
    )(
        order,
        packed,
        packed,
        select,
        shifts,
        edges,
        before,
        at_end,
        causal,
        history,
        history_state,
        taps,
        taps_state,
        skip_lanes,
        bias,
        rate,
        state_pool,
    )


def by_chunk(array, chunks, lanes):
    rows, width = array.shape
    parts = array.reshape(rows, chunks, width // chunks).transpose(1, 0, 2)
    return jnp.pad(parts, ((0, 0), (0, 0), (0, lanes - width // chunks)))


def spread_weight(weight, chunks):
    me = lax.axis_index("slab")
    pieces = [
        rotate(lax.dynamic_index_in_dim(weight, (me + step) % chunks, 0, keepdims=False), "slab", step)
        for step in range(chunks)
    ]
    full = place(pieces, [(me - step) % chunks for step in range(chunks)])
    full = full.reshape(-1, full.shape[2])
    full = gather_axis(full, "side", 0)
    return gather_axis(full, "core", 0)


def on_device(
    hidden_in,
    z_weight,
    x_weight,
    state_proj,
    step_weight,
    step_bias,
    decay_log,
    skip_gain,
    conv_inner,
    conv_state,
    norm_gain,
    out_weight,
    state_pool,
    conv_pool_inner,
    conv_pool_state,
    owner_dev,
    state_page,
    conv_page,
    accepted,
):
    groups = lax.axis_size(RING)
    chunks, sides, cores = (lax.axis_size(name) for name in RING)
    this_dev = lax.axis_index(RING)
    me = lax.axis_index("slab")
    splits = lax.axis_size("mdl")
    part = lax.axis_index("mdl")
    per_dev, all_heads, head_dim, state_width = state_pool.shape
    rows, depth = hidden_in.shape
    draft = rows // per_dev
    inner = all_heads * head_dim
    slots = WINDOW * CAP
    chunk_width = inner // chunks
    lanes = round_up(chunk_width, LANES)
    map_width = 2 * state_width // chunks
    heads = all_heads // chunks
    aux_lanes = round_up(map_width + heads, LANES)
    keep = KCONV - 1
    hist_rows = per_dev * keep
    hist_pad = round_up(hist_rows, 32)

    send_table, gather_table, conv_of, kept_count = route_tables(
        owner_dev, state_page, conv_page, accepted, groups, per_dev, this_dev
    )

    block = depth // groups
    columns = hidden_in.reshape(rows, chunks, sides, cores, block).transpose(0, 3, 2, 1, 4)
    columns = columns.reshape(rows, splits, depth // splits)
    share = lax.dynamic_index_in_dim(columns, part, 1, keepdims=False)
    outgoing = one_hot_apply(send_table, share, (slots, draft, depth // splits))
    incoming = jnp.concatenate(
        [
            rotate(outgoing[offset * CAP : (offset + 1) * CAP], RING, offset)
            for offset in range(WINDOW)
        ],
        axis=0,
    )
    owned = one_hot_apply(gather_table, incoming, (rows, depth // splits))
    owned_all = jnp.stack([rotate(owned, "slab", step) for step in range(chunks)])
    owned_all = gather_axis(owned_all, "mdl", 2)

    packed_weight = jnp.concatenate(
        [
            by_chunk(x_weight, chunks, lanes),
            by_chunk(state_proj, chunks, map_width),
            by_chunk(step_weight, chunks, aux_lanes - map_width),
        ],
        axis=2,
    )
    packed_full = spread_weight(packed_weight, chunks)
    gate_full = spread_weight(by_chunk(z_weight, chunks, lanes), chunks)
    out_full = lax.all_gather(out_weight, RING, axis=1, tiled=True)

    owned_flat = owned_all.reshape(chunks * rows, depth)
    packed = jnp.dot(owned_flat, packed_full, preferred_element_type=F32).astype(BF16)
    packed = packed.reshape(chunks, rows, lanes + aux_lanes)
    packed = jnp.stack([rotate(packed[step], "slab", -step) for step in range(chunks)])
    gate = jnp.dot(owned_flat, gate_full, preferred_element_type=F32).astype(BF16)
    gate = gate.reshape(chunks, rows, lanes)
    gate = jnp.stack([rotate(gate[step], "slab", -step) for step in range(chunks)])

    order = (jnp.arange(chunks, dtype=jnp.int32) - me) % chunks
    home_chunk = (jnp.arange(chunks, dtype=jnp.int32) + me) % chunks
    lane = jnp.arange(aux_lanes, dtype=jnp.int32)[None, :]
    step_lanes = round_up(all_heads, LANES)
    target = jnp.where(
        lane < map_width,
        home_chunk[:, None] * map_width + lane,
        jnp.where(
            lane < map_width + heads,
            2 * state_width + home_chunk[:, None] * heads + lane - map_width,
            -1,
        ),
    )
    select = (
        target[:, :, None] == jnp.arange(2 * state_width + step_lanes, dtype=jnp.int32)
    ).astype(BF16)
    tables = series_tables(conv_of, kept_count, per_dev, draft, hist_pad)
    pad_rows = ((0, hist_pad - hist_rows), (0, 0))
    history = by_chunk(
        jnp.pad(conv_pool_inner.reshape(hist_rows, inner), pad_rows), chunks, lanes
    )
    history_state = jnp.pad(conv_pool_state.reshape(hist_rows, 2 * state_width), pad_rows)
    pad_heads = (0, step_lanes - all_heads)
    y_rows, new_states, conv_rows, conv_state_rows = mix_requests(
        packed,
        order,
        select,
        tables,
        history,
        history_state,
        by_chunk(conv_inner, chunks, lanes),
        conv_state,
        by_chunk(jnp.repeat(skip_gain, head_dim)[None], chunks, lanes),
        jnp.pad(step_bias, pad_heads)[None],
        jnp.pad(-jnp.exp(decay_log), pad_heads)[None],
        state_pool,
    )

    gate_here = jnp.roll(gate, me, axis=0).astype(F32)[:, :, :chunk_width]
    gated = y_rows[:, :, :chunk_width].astype(F32) * (gate_here / (1.0 + jnp.exp(-gate_here)))
    squares = jnp.sum(gated * gated, axis=(0, 2))
    scaled = (gated * norm_gain.reshape(chunks, 1, chunk_width)).astype(BF16)
    scaled = scaled.transpose(1, 0, 2).reshape(rows, inner)
    terms = jnp.dot(scaled, out_full, preferred_element_type=F32)
    wide = depth // splits
    if splits == 2:
        squares = squares + rotate(squares, "mdl", 1)
        mine = lax.dynamic_slice_in_dim(terms, part * wide, wide, 1)
        other = lax.dynamic_slice_in_dim(terms, (1 - part) * wide, wide, 1)
        total = mine + rotate(other.astype(BF16), "mdl", 1).astype(F32)
    else:
        squares = lax.psum(squares, "mdl")
        total = lax.psum_scatter(terms, "mdl", scatter_dimension=1, tiled=True)
    scale = lax.rsqrt(squares / (inner * splits) + EPSILON)
    mixed_rows = (total * scale[:, None]).astype(BF16)

    returning = one_hot_apply(
        gather_table.T, mixed_rows.reshape(per_dev, draft, wide), (slots, draft, wide)
    )
    arrived = jnp.concatenate(
        [
            rotate(returning[offset * CAP : (offset + 1) * CAP], RING, -offset)
            for offset in range(WINDOW)
        ],
        axis=0,
    )
    mixed = one_hot_apply(send_table.T, arrived, (rows, wide))
    conv_rows = conv_rows[:, :hist_rows, :chunk_width].transpose(1, 0, 2)
    return (
        mixed,
        new_states,
        conv_rows.reshape(per_dev, keep, inner),
        conv_state_rows[:hist_rows].reshape(per_dev, keep, 2 * state_width),
    )


def solution(mesh):
    slab, side, core = factor(mesh.shape["req"])
    split_mesh = Mesh(
        mesh.devices.reshape(slab, side, core, mesh.shape["mdl"]), RING + ("mdl",)
    )
    return jax.shard_map(
        on_device,
        mesh=split_mesh,
        in_specs=(
            P(RING, None),
            P(RING, "mdl"),
            P(RING, "mdl"),
            P(RING, None),
            P(RING, "mdl"),
            P("mdl"),
            P("mdl"),
            P("mdl"),
            P(None, "mdl"),
            P(),
            P("mdl"),
            P("mdl", RING),
            P(RING, "mdl", None, None),
            P(RING, None, "mdl"),
            P(RING, None, None),
            P(),
            P(),
            P(),
            P(),
        ),
        out_specs=(
            P(RING, "mdl"),
            P(RING, "mdl", None, None),
            P(RING, None, "mdl"),
            P(RING, None, None),
        ),
        check_vma=False,
    )
```

```python
import jax
import jax.numpy as jnp
from jax import lax
from jax.experimental import pallas as pl
from jax.experimental.pallas import tpu as pltpu
from jax.sharding import Mesh, PartitionSpec as P

KCONV = 4
CAP = 2
WINDOW = 8
LANES = 128
QUICK = pl.CostEstimate(flops=1000, bytes_accessed=1000, transcendentals=0)
VMEM_LIMIT = 56 * 1024 * 1024
EPSILON = 1e-05
HIGH = lax.Precision.HIGHEST
BF16 = jnp.bfloat16
F32 = jnp.float32

RING = ("far", "near", "side", "core")
SLABS = ("far", "near")


def round_up(value, unit):
    return -(-value // unit) * unit


def factor(count):
    core, near = 2, 2
    chips = count // core
    side = 1
    while (2 * side) ** 2 <= chips:
        side *= 2
    return chips // side // near, near, side, core


def rotate(value, axis, steps):
    count = lax.axis_size(axis)
    if steps % count == 0:
        return value
    pairs = [(source, (source + steps) % count) for source in range(count)]
    return lax.ppermute(value, axis, pairs)


def gather_axis(value, axis, dim):
    count = lax.axis_size(axis)
    if count == 1:
        return value
    if count > 2:
        return lax.all_gather(value, axis, axis=dim, tiled=True)
    peer = rotate(value, axis, 1)
    first = lax.axis_index(axis) == 0
    return jnp.concatenate(
        [jnp.where(first, value, peer), jnp.where(first, peer, value)], axis=dim
    )


def place(pieces, slots):
    full = jnp.zeros((len(pieces),) + pieces[0].shape, pieces[0].dtype)
    for piece, slot in zip(pieces, slots):
        full = lax.dynamic_update_slice_in_dim(full, piece[None], slot, 0)
    return full


def one_hot_apply(table, values, shape):
    flat = values.reshape(table.shape[1], -1)
    return jnp.dot(table, flat, preferred_element_type=F32).astype(BF16).reshape(shape)


def route_tables(owner_dev, state_page, conv_page, accepted, groups, per_dev, this_dev):
    owner_grid = owner_dev.reshape(groups, per_dev)
    home_grid = jnp.arange(groups, dtype=jnp.int32)[:, None]
    offset_grid = (owner_grid - home_grid + groups) % groups
    positions = jnp.arange(per_dev, dtype=jnp.int32)
    earlier = positions[None, :] < positions[:, None]
    pair_rank = jnp.sum((owner_grid[:, :, None] == owner_grid[:, None, :]) & earlier[None], axis=2)
    slot_grid = offset_grid * CAP + pair_rank
    send_at = lax.dynamic_slice_in_dim(slot_grid, this_dev, 1, 0)[0]
    buffer_rows = jnp.arange(WINDOW * CAP, dtype=jnp.int32)
    send_table = (buffer_rows[:, None] == send_at[None, :]).astype(BF16)
    arrive_at = slot_grid.reshape(-1)
    slot_match = (owner_dev[None, :] == this_dev) & (state_page[None, :] == positions[:, None])
    pick_from = jnp.sum(jnp.where(slot_match, arrive_at[None, :], 0), axis=1)
    conv_of = jnp.sum(jnp.where(slot_match, conv_page[None, :], 0), axis=1)
    kept_count = jnp.sum(jnp.where(slot_match, accepted[None, :], 0), axis=1)
    gather_table = (buffer_rows[None, :] == pick_from[:, None]).astype(BF16)
    return (send_table, gather_table, conv_of, kept_count)


def tables_kernel(sizes, conv_ref, kept_ref, moves_ref, masks_ref):
    per_dev, draft, hist_pad = sizes
    rows = per_dev * draft
    keep = KCONV - 1
    width = rows + hist_pad

    def pick(slot, scalars):
        return sum(jnp.where(slot == at, scalars[at], 0) for at in range(per_dev))

    row = lax.broadcasted_iota(jnp.int32, (rows, width), 0)
    column = lax.broadcasted_iota(jnp.int32, (rows, width), 1)
    step = row % draft
    page_row = pick(row // draft, conv_ref) * keep
    for delay in range(1, KCONV):
        source = jnp.where(step >= delay, row - delay, rows + page_row + keep + step - delay)
        moves_ref[(delay - 1) * rows : delay * rows, :] = (column == source).astype(F32).astype(BF16)
    out_row = lax.broadcasted_iota(jnp.int32, (hist_pad, width), 0)
    column = lax.broadcasted_iota(jnp.int32, (hist_pad, width), 1)
    out_page, out_at = out_row // keep, out_row % keep
    source = jnp.full((hist_pad, width), -1, jnp.int32)
    for slot in range(per_dev):
        at = kept_ref[slot] + out_at
        held = jnp.where(at < keep, rows + out_page * keep + at, slot * draft + at - keep)
        source = jnp.where(out_page == conv_ref[slot], held, source)
    moves_ref[keep * rows : keep * rows + hist_pad, :] = (column == source).astype(F32).astype(BF16)
    row = lax.broadcasted_iota(jnp.int32, (rows, rows), 0)
    column = lax.broadcasted_iota(jnp.int32, (rows, rows), 1)
    step = row % draft
    kept = pick(row // draft, kept_ref)
    masks_ref[0] = (step < kept).astype(F32)
    masks_ref[1] = (column == row - step + kept - 1).astype(F32)
    masks_ref[2] = ((row // draft == column // draft) & (column <= row)).astype(F32)


def series_tables(conv_of, kept_count, per_dev, draft, hist_pad):
    rows = per_dev * draft
    smem = pl.BlockSpec(memory_space=pltpu.SMEM)
    return pl.pallas_call(
        lambda *refs: tables_kernel((per_dev, draft, hist_pad), *refs),
        in_specs=[smem, smem],
        out_specs=[pl.BlockSpec(memory_space=pltpu.VMEM)] * 2,
        out_shape=[
            jax.ShapeDtypeStruct(((KCONV - 1) * rows + hist_pad, rows + hist_pad), BF16),
            jax.ShapeDtypeStruct((3, rows, rows), F32),
        ],
    )(conv_of, kept_count)


def split_pair(value):
    high = value.astype(BF16)
    return high, (value - high.astype(F32)).astype(BF16)


def convolve(series, current, taps, moves_ref):
    rows = current.shape[0]
    total = taps[KCONV - 1 : KCONV] * current
    for delay in range(1, KCONV):
        move = moves_ref[(delay - 1) * rows : delay * rows, :]
        moved = jnp.dot(move, series, preferred_element_type=F32)
        total = total + taps[KCONV - 1 - delay : KCONV - delay] * moved
    return total / (1.0 + jnp.exp(-total))


def mixer_kernel(
    sizes,
    order_ref,
    *refs,
):
    chunks, per_dev, draft, heads, head_dim, state_width = sizes
    x_refs, aux_refs, refs = refs[:chunks], refs[chunks : 2 * chunks], refs[2 * chunks :]
    (
        select_ref,
        moves_ref,
        masks_ref,
        hist_ref,
        hist_state_ref,
        taps_ref,
        taps_state_ref,
        skip_ref,
        step_ref,
        state_ref,
        y_ref,
        new_state_ref,
        conv_ref,
        conv_state_ref,
        b_scr,
        c_scr,
        scores_scr,
        log_scr,
        sel_scr,
        end_scr,
        log_t_scr,
        step_t_scr,
    ) = refs
    rows = per_dev * draft
    width = heads * head_dim
    group = pl.program_id(0)
    causal = masks_ref[2]
    edges = moves_ref[(KCONV - 1) * rows :, :]

    @pl.when(group == 0)
    def prepare():
        aux = jnp.dot(aux_refs[0][...], select_ref[0], preferred_element_type=F32)
        for chunk in range(1, chunks):
            aux = aux + jnp.dot(aux_refs[chunk][...], select_ref[chunk], preferred_element_type=F32)
        maps = aux[:, : 2 * state_width]
        series = jnp.concatenate([maps.astype(BF16), hist_state_ref[...]], axis=0)
        active = convolve(series, maps, taps_state_ref[...], moves_ref)
        conv_state_ref[...] = jnp.dot(edges, series, preferred_element_type=F32).astype(BF16)
        b_rows, c_rows = active[:, :state_width], active[:, state_width:]
        b_scr[...] = b_rows
        c_scr[...] = c_rows
        scores_scr[...] = lax.dot_general(
            c_rows, b_rows, (((1,), (1,)), ((), ())), precision=HIGH, preferred_element_type=F32
        ) * causal
        raw = aux[:, 2 * state_width :] + step_ref[:1, :]
        step_size = jnp.maximum(raw, 0.0) + jnp.log1p(jnp.exp(-jnp.abs(raw)))
        log_decay = jnp.dot(causal, step_size * step_ref[1:2, :], precision=HIGH, preferred_element_type=F32)
        end = jnp.dot(masks_ref[1], log_decay, precision=HIGH, preferred_element_type=F32)
        kept = masks_ref[0] > 0.0
        chosen = jnp.where(kept, jnp.exp(jnp.where(kept, end - log_decay, 0.0)), 0.0) * step_size
        decay_end = jnp.exp(end)
        for chunk in range(chunks):
            part = slice(chunk * heads, (chunk + 1) * heads)
            log_scr[chunk] = log_decay[:, part]
            sel_scr[chunk] = chosen[:, part]
            end_scr[chunk] = decay_end[:, part]
        log_t_scr[...] = log_decay.T
        step_t_scr[...] = step_size.T

    x_rows = x_refs[0][...]
    for chunk in range(1, chunks):
        x_rows = jnp.where(order_ref[group] == chunk, x_refs[chunk][...], x_rows)
    series = jnp.concatenate([x_rows, hist_ref[...]], axis=0)
    active = convolve(series, x_rows.astype(F32), taps_ref[...], moves_ref)
    conv_ref[...] = jnp.dot(edges, series, preferred_element_type=F32).astype(BF16)
    scores = scores_scr[...]
    log_here = log_scr[group]
    sel_here = sel_scr[group]
    end_here = end_scr[group]
    within, growth, picks = [], [], []
    for head in range(heads):
        lanes = slice(head * head_dim, (head + 1) * head_dim)
        at = group * heads + head
        log_row = log_t_scr[pl.ds(at, 1), :]
        step_row = step_t_scr[pl.ds(at, 1), :]
        spread = jnp.where(causal > 0.0, log_here[:, head : head + 1] - log_row, -1e30)
        weight = jnp.exp(spread) * (scores * step_row)
        x_head = active[:, lanes]
        within.append(
            jnp.dot(weight.astype(BF16), x_head.astype(BF16), preferred_element_type=F32)
            + skip_ref[at] * x_head
        )
        growth.append(jnp.broadcast_to(jnp.exp(log_here[:, head : head + 1]), (rows, head_dim)))
        picks.append(jnp.broadcast_to(sel_here[:, head : head + 1], (rows, head_dim)))
    within = jnp.concatenate(within, axis=1)
    growth = jnp.concatenate(growth, axis=1)
    picked = active * jnp.concatenate(picks, axis=1)
    carried = []
    for slot in range(per_dev):
        part = slice(slot * draft, (slot + 1) * draft)
        state = state_ref[slot].reshape(width, state_width)
        carried.append(
            lax.dot_general(
                c_scr[part, :].astype(BF16),
                state.astype(BF16),
                (((1,), (1,)), ((), ())),
                preferred_element_type=F32,
            )
        )
        x_high, x_low = split_pair(picked[part])
        b_high, b_low = split_pair(b_scr[part, :])
        update = lax.dot_general(
            jnp.concatenate([x_high, x_low, x_high], axis=0),
            jnp.concatenate([b_high, b_high, b_low], axis=0),
            (((0,), (0,)), ((), ())),
            preferred_element_type=F32,
        )
        for head in range(heads):
            keep = end_here[slot * draft : slot * draft + 1, head : head + 1]
            lanes = slice(head * head_dim, (head + 1) * head_dim)
            new_state_ref[slot, head] = keep * state[lanes] + update[lanes]
    carried = jnp.concatenate(carried, axis=0)
    y_ref[...] = (within + growth * carried).astype(BF16)


def mix_requests(
    packed,
    order,
    select,
    tables,
    history,
    history_state,
    taps,
    taps_state,
    skip_gain,
    steps,
    state_pool,
):
    rows, packed_width = packed[0].shape
    chunks = len(packed)
    per_dev, all_heads, head_dim, state_width = state_pool.shape
    hist_pad, inner = history.shape
    heads = all_heads // chunks
    draft = rows // per_dev
    lanes = inner // chunks
    aux_lanes = packed_width - lanes
    moves, masks = tables
    sizes = (chunks, per_dev, draft, heads, head_dim, state_width)

    def whole(array):
        zeros = (0,) * array.ndim
        return pl.BlockSpec(array.shape, lambda group, order_ref: zeros)

    def by_group(height):
        return pl.BlockSpec((height, lanes), lambda group, order_ref: (0, group))

    x_spec = pl.BlockSpec((rows, lanes), lambda group, order_ref: (0, 0))
    aux_spec = pl.BlockSpec(
        (rows, aux_lanes), lambda group, order_ref: (0, lanes // aux_lanes)
    )

    state_spec = pl.BlockSpec(
        (per_dev, heads, head_dim, state_width), lambda group, order_ref: (0, group, 0, 0)
    )
    step_lanes = select.shape[2] - 2 * state_width
    grid_spec = pltpu.PrefetchScalarGridSpec(
        num_scalar_prefetch=1,
        grid=(chunks,),
        in_specs=[
            *[x_spec] * chunks,
            *[aux_spec] * chunks,
            whole(select),
            whole(moves),
            whole(masks),
            by_group(hist_pad),
            whole(history_state),
            by_group(KCONV),
            whole(taps_state),
            pl.BlockSpec(memory_space=pltpu.SMEM),
            whole(steps),
            state_spec,
        ],
        out_specs=[
            by_group(rows),
            state_spec,
            by_group(hist_pad),
            pl.BlockSpec((hist_pad, 2 * state_width), lambda group, order_ref: (0, 0)),
        ],
        scratch_shapes=[
            pltpu.VMEM((rows, state_width), F32),
            pltpu.VMEM((rows, state_width), F32),
            pltpu.VMEM((rows, rows), F32),
            pltpu.VMEM((chunks, rows, heads), F32),
            pltpu.VMEM((chunks, rows, heads), F32),
            pltpu.VMEM((chunks, rows, heads), F32),
            pltpu.VMEM((step_lanes, rows), F32),
            pltpu.VMEM((step_lanes, rows), F32),
        ],
    )
    return pl.pallas_call(
        lambda *refs: mixer_kernel(sizes, *refs),
        grid_spec=grid_spec,
        out_shape=(
            jax.ShapeDtypeStruct((rows, inner), BF16),
            jax.ShapeDtypeStruct(state_pool.shape, F32),
            jax.ShapeDtypeStruct((hist_pad, inner), BF16),
            jax.ShapeDtypeStruct((hist_pad, 2 * state_width), BF16),
        ),
        compiler_params=pltpu.CompilerParams(vmem_limit_bytes=VMEM_LIMIT),
        cost_estimate=pl.CostEstimate(
            flops=64 * rows * rows * all_heads * head_dim,
            bytes_accessed=8 * state_pool.size,
            transcendentals=rows * rows * all_heads,
        ),
    )(
        order,
        *packed,
        *packed,
        select,
        moves,
        masks,
        history,
        history_state,
        taps,
        taps_state,
        skip_gain,
        steps,
        state_pool,
    )


def by_chunk(array, chunks, lanes):
    rows, width = array.shape
    parts = array.reshape(rows, chunks, width // chunks).transpose(1, 0, 2)
    return jnp.pad(parts, ((0, 0), (0, 0), (0, lanes - width // chunks)))


def swap(value, axis):
    return rotate(value, axis, 1)


def near_half(weight):
    me = lax.axis_index("near")
    keep = lax.dynamic_index_in_dim(weight, me, 0, keepdims=False)
    give = lax.dynamic_index_in_dim(weight, 1 - me, 0, keepdims=False)
    take = swap(give, "near")
    return jnp.concatenate([jnp.where(me == 0, keep, take), jnp.where(me == 0, take, keep)])


def tie(value, *others):
    return lax.optimization_barrier((value,) + others)[0]


def out_kernel(place_ref, own_ref, peer_ref, *refs):
    weight_refs, out_ref = refs[:8], refs[8]
    rows = own_ref.shape[0]
    both = jnp.concatenate([own_ref[...], peer_ref[...]], axis=0)
    for pair in range(4):
        weight = jnp.concatenate([weight_refs[2 * pair][...], weight_refs[2 * pair + 1][...]], axis=1)
        total = jnp.dot(both, weight, preferred_element_type=F32)
        for at in range(2):
            start = place_ref[(2 * pair + at) % 4] * LANES
            lanes = pl.ds(pl.multiple_of(start, LANES), LANES)
            out_ref[pair // 2, :, lanes] = total[:, at * LANES : (at + 1) * LANES]


def project_out(own, peer, weights, place_of):
    rows, depth = own.shape
    whole = pl.BlockSpec(memory_space=pltpu.VMEM)
    return pl.pallas_call(
        out_kernel,
        in_specs=[pl.BlockSpec(memory_space=pltpu.SMEM)] + [whole] * 10,
        out_specs=whole,
        out_shape=jax.ShapeDtypeStruct((2, 2 * rows, 4 * LANES), F32),
        compiler_params=pltpu.CompilerParams(vmem_limit_bytes=24 * 1024 * 1024),
        cost_estimate=QUICK,
    )(place_of, own, peer, *weights)


def on_device(
    hidden_in,
    z_weight,
    x_weight,
    state_proj,
    step_weight,
    step_bias,
    decay_log,
    skip_gain,
    conv_inner,
    conv_state,
    norm_gain,
    out_weight,
    state_pool,
    conv_pool_inner,
    conv_pool_state,
    owner_dev,
    state_page,
    conv_page,
    accepted,
):
    groups = lax.axis_size(RING)
    fars, nears, sides, cores = (lax.axis_size(name) for name in RING)
    splits = lax.axis_size("mdl")
    paired = (fars, nears, sides, cores, splits) == (2, 2, 2, 2, 2)
    paired = paired and hidden_in.shape[1] == groups * LANES
    chunks = fars * nears if paired else nears
    this_dev = lax.axis_index(RING)
    near_at = lax.axis_index("near")
    me = lax.axis_index(SLABS) if paired else near_at
    part = lax.axis_index("mdl")
    per_dev, all_heads, head_dim, state_width = state_pool.shape
    rows, depth = hidden_in.shape
    draft = rows // per_dev
    inner = all_heads * head_dim
    slots = WINDOW * CAP
    chunk_width = inner // chunks
    lanes = chunk_width
    map_width = 2 * state_width // chunks
    heads = all_heads // chunks
    aux_lanes = round_up(map_width + heads, LANES)
    keep = KCONV - 1
    hist_rows = per_dev * keep
    hist_pad = round_up(hist_rows, 32)

    send_table, gather_table, conv_of, kept_count = route_tables(
        owner_dev, state_page, conv_page, accepted, groups, per_dev, this_dev
    )

    order = (jnp.arange(chunks, dtype=jnp.int32) - me) % chunks
    home_chunk = (jnp.arange(chunks, dtype=jnp.int32) + me) % chunks
    lane = jnp.arange(aux_lanes, dtype=jnp.int32)[None, :]
    step_lanes = round_up(all_heads, LANES)
    target = jnp.where(
        lane < map_width,
        home_chunk[:, None] * map_width + lane,
        jnp.where(
            lane < map_width + heads,
            2 * state_width + home_chunk[:, None] * heads + lane - map_width,
            -1,
        ),
    )
    select = (
        target[:, :, None] == jnp.arange(2 * state_width + step_lanes, dtype=jnp.int32)
    ).astype(BF16)
    tables = series_tables(conv_of, kept_count, per_dev, draft, hist_pad)
    pad_rows = ((0, hist_pad - hist_rows), (0, 0))
    history = jnp.pad(conv_pool_inner.reshape(hist_rows, inner), pad_rows)
    history_state = jnp.pad(conv_pool_state.reshape(hist_rows, 2 * state_width), pad_rows)
    pad_heads = ((0, 0), (0, step_lanes - all_heads))
    steps = jnp.pad(jnp.stack([step_bias, -jnp.exp(decay_log)]), pad_heads)


    block = depth // groups
    columns = hidden_in.reshape(rows, fars, nears, sides, cores, block).transpose(0, 4, 3, 1, 2, 5)
    columns = columns.reshape(rows, splits, depth // splits)
    share = lax.dynamic_index_in_dim(columns, part, 1, keepdims=False)
    outgoing = one_hot_apply(send_table, share, (slots, draft, depth // splits))
    incoming = [
        rotate(outgoing[offset * CAP : (offset + 1) * CAP], RING, offset) for offset in range(WINDOW)
    ]

    packed_weight = jnp.concatenate(
        [
            by_chunk(x_weight, chunks, lanes),
            by_chunk(state_proj, chunks, map_width),
            by_chunk(step_weight, chunks, aux_lanes - map_width),
            by_chunk(z_weight, chunks, lanes),
        ],
        axis=2,
    )
    split = lanes + aux_lanes
    width = split + lanes
    far, side, core = (lax.axis_index(name) for name in ("far", "side", "core"))
    if paired:
        pieces = [
            rotate(
                lax.dynamic_index_in_dim(packed_weight, (me + step) % chunks, 0, keepdims=False),
                SLABS,
                step,
            )
            for step in range(chunks)
        ]
        across = swap(pieces[0], "side")
        incoming, pieces, across, select, history, history_state, steps, tables = (
            lax.optimization_barrier(
                (incoming, pieces, across, select, history, history_state, steps, tables)
            )
        )
        owned = one_hot_apply(gather_table, jnp.concatenate(incoming), (rows, depth // splits))
        owned, pieces = lax.optimization_barrier((owned, pieces))
        rows_of = [rotate(owned, SLABS, step) for step in range(chunks)]
        rows_peer = swap(owned, "mdl")
        slabs = [(me - step) % chunks for step in range(chunks)]
        held = place(pieces, slabs)
        across = place([across] + [swap(piece, "side") for piece in pieces[1:]], slabs)
        rows_of, rows_peer, across, held = lax.optimization_barrier((rows_of, rows_peer, across, held))
        rows_rest = swap(jnp.stack(rows_of[1:]), "mdl")
        at_core, at_side, at_half = core == 0, side == 0, part == 0
        held_peer, across_peer = swap(held, "core"), swap(across, "core")

        def full(columns):
            own = [value[:, :, columns].reshape(-1, columns.stop - columns.start) for value in (held, across)]
            peer = [
                value[:, :, columns].reshape(-1, columns.stop - columns.start)
                for value in (held_peer, across_peer)
            ]
            parts = []
            for first, second in ((own, peer), (peer, own)):
                low = [jnp.where(at_core, first[at], second[at]) for at in range(2)]
                parts += [jnp.where(at_side, low[0], low[1]), jnp.where(at_side, low[1], low[0])]
            return jnp.concatenate(parts)

        packed_full, gate_full = full(slice(0, split)), full(slice(split, width))
        out_far, out_side = swap(out_weight, "far"), swap(out_weight, "side")
        rows_rest, packed_full, gate_full, out_far, out_side = lax.optimization_barrier(
            (rows_rest, packed_full, gate_full, out_far, out_side)
        )
        own_rows = jnp.concatenate(rows_of)
        peer_rows = jnp.concatenate([rows_peer, rows_rest.reshape(-1, depth // splits)])
        all_rows = jnp.concatenate(
            [jnp.where(at_half, own_rows, peer_rows), jnp.where(at_half, peer_rows, own_rows)], axis=1
        )
        packed = jnp.dot(all_rows, packed_full, preferred_element_type=F32).astype(BF16)
        packed = packed.reshape(chunks, rows, split)
        packed = [rotate(packed[step], SLABS, -step) for step in range(chunks)]
        gate = jnp.dot(all_rows, gate_full, preferred_element_type=F32).astype(BF16)
        gate = gate.reshape(chunks, rows, lanes)
        out_across = swap(out_far, "side")
        packed, gate, out_across = lax.optimization_barrier((packed, gate, out_across))
        gate = [rotate(gate[step], SLABS, -step) for step in range(chunks)]
        out_columns = []
        for column in (out_weight, out_side, out_far, out_across):
            out_columns += [column, swap(column, "core")]
    else:
        owned = one_hot_apply(gather_table, jnp.concatenate(incoming), (rows, depth // splits))
        owned = lax.all_gather(owned, "mdl", axis=1, tiled=True)
        owned = jnp.concatenate([owned, swap(owned, "near")])
        weight = near_half(packed_weight)
        for name in ("far", "side", "core"):
            weight = lax.all_gather(weight, name, axis=0, tiled=True)
        total = jnp.dot(owned, weight, preferred_element_type=F32).astype(BF16)
        total = [total[:rows], swap(total[rows:], "near")]
        packed = [value[:, :split] for value in total]
        gate = [value[:, split:] for value in total]
        out_columns = lax.all_gather(out_weight, RING, axis=1, tiled=True)

    y_rows, new_states, conv_rows, conv_state_rows = mix_requests(
        packed,
        order,
        select,
        tables,
        history,
        history_state,
        conv_inner,
        conv_state,
        skip_gain,
        steps,
        state_pool,
    )

    gate_here = []
    for chunk in range(chunks):
        value = gate[0]
        for step in range(1, chunks):
            value = jnp.where(me == (chunk - step) % chunks, gate[step], value)
        gate_here.append(value)
    gate_here = jnp.concatenate(gate_here, axis=1).astype(F32)
    gated = y_rows.astype(F32) * (gate_here / (1.0 + jnp.exp(-gate_here)))
    squares = jnp.sum(gated * gated, axis=1)
    scaled = (gated * norm_gain).astype(BF16)
    wide = depth // splits
    total_inner = inner * splits
    if paired:
        squares = squares + swap(squares, "mdl")
        scale = lax.rsqrt(squares / total_inner + EPSILON)
        scale = jnp.concatenate([scale, swap(scale, "near")])
        columns_at = jnp.stack(
            [2 * at_side + at_core for at_side in (side, 1 - side) for at_core in (core, 1 - core)]
        )
        terms = project_out(scaled, swap(scaled, "near"), out_columns, columns_at)
        here = far == part
        mine = jnp.where(here, terms[0], terms[1])
        other = jnp.where(here, terms[1], terms[0]).astype(BF16)
        total = (mine + swap(other, "mdl").astype(F32)) * scale[:, None]
        total = total.astype(BF16).reshape(2, rows, wide // 2)
        given = swap(total[1], "near")
        mixed_rows = jnp.concatenate(
            [jnp.where(near_at == 0, total[0], given), jnp.where(near_at == 0, given, total[0])], axis=1
        )
    else:
        terms = jnp.dot(scaled, out_columns, preferred_element_type=F32)
        squares = lax.psum(squares, "mdl")
        total = lax.psum_scatter(terms, "mdl", scatter_dimension=1, tiled=True)
        scale = lax.rsqrt(squares / total_inner + EPSILON)
        mixed_rows = (total * scale[:, None]).astype(BF16)

    returning = one_hot_apply(
        gather_table.T, mixed_rows.reshape(per_dev, draft, wide), (slots, draft, wide)
    )
    arrived = jnp.concatenate(
        [
            rotate(returning[offset * CAP : (offset + 1) * CAP], RING, -offset)
            for offset in range(WINDOW)
        ],
        axis=0,
    )
    mixed = one_hot_apply(send_table.T, arrived, (rows, wide))
    return (
        mixed,
        new_states,
        conv_rows[:hist_rows].reshape(per_dev, keep, inner),
        conv_state_rows[:hist_rows].reshape(per_dev, keep, 2 * state_width),
    )


def solution(mesh):
    sizes = factor(mesh.shape["req"])
    split_mesh = Mesh(mesh.devices.reshape(*sizes, mesh.shape["mdl"]), RING + ("mdl",))
    return jax.shard_map(
        on_device,
        mesh=split_mesh,
        in_specs=(
            P(RING, None),
            P(RING, "mdl"),
            P(RING, "mdl"),
            P(RING, None),
            P(RING, "mdl"),
            P("mdl"),
            P("mdl"),
            P("mdl"),
            P(None, "mdl"),
            P(),
            P("mdl"),
            P("mdl", RING),
            P(RING, "mdl", None, None),
            P(RING, None, "mdl"),
            P(RING, None, None),
            P(),
            P(),
            P(),
            P(),
        ),
        out_specs=(
            P(RING, "mdl"),
            P(RING, "mdl", None, None),
            P(RING, None, "mdl"),
            P(RING, None, None),
        ),
        check_vma=False,
    )
```

```python
import jax
import jax.numpy as jnp
from jax import lax
from jax.experimental import pallas as pl
from jax.experimental.pallas import tpu as pltpu
from jax.sharding import Mesh, PartitionSpec as P

KCONV = 4
CAP = 2
WINDOW = 8
LANES = 128
QUICK = pl.CostEstimate(flops=1000, bytes_accessed=1000, transcendentals=0)
VMEM_LIMIT = 56 * 1024 * 1024
EPSILON = 1e-05
HIGH = lax.Precision.HIGHEST
BF16 = jnp.bfloat16
F32 = jnp.float32

RING = ("far", "near", "side", "core")
SLABS = ("far", "near")


def round_up(value, unit):
    return -(-value // unit) * unit


def factor(count):
    core, near = 2, 2
    chips = count // core
    side = 1
    while (2 * side) ** 2 <= chips:
        side *= 2
    return chips // side // near, near, side, core


def rotate(value, axis, steps):
    count = lax.axis_size(axis)
    if steps % count == 0:
        return value
    pairs = [(source, (source + steps) % count) for source in range(count)]
    return lax.ppermute(value, axis, pairs)


def gather_axis(value, axis, dim):
    count = lax.axis_size(axis)
    if count == 1:
        return value
    if count > 2:
        return lax.all_gather(value, axis, axis=dim, tiled=True)
    peer = rotate(value, axis, 1)
    first = lax.axis_index(axis) == 0
    return jnp.concatenate(
        [jnp.where(first, value, peer), jnp.where(first, peer, value)], axis=dim
    )


def place(pieces, slots):
    full = jnp.zeros((len(pieces),) + pieces[0].shape, pieces[0].dtype)
    for piece, slot in zip(pieces, slots):
        full = lax.dynamic_update_slice_in_dim(full, piece[None], slot, 0)
    return full


def one_hot_apply(table, values, shape):
    flat = values.reshape(table.shape[1], -1)
    return jnp.dot(table, flat, preferred_element_type=F32).astype(BF16).reshape(shape)


def route_tables(owner_dev, state_page, conv_page, accepted, groups, per_dev, this_dev):
    owner_grid = owner_dev.reshape(groups, per_dev)
    home_grid = jnp.arange(groups, dtype=jnp.int32)[:, None]
    offset_grid = (owner_grid - home_grid + groups) % groups
    positions = jnp.arange(per_dev, dtype=jnp.int32)
    earlier = positions[None, :] < positions[:, None]
    pair_rank = jnp.sum((owner_grid[:, :, None] == owner_grid[:, None, :]) & earlier[None], axis=2)
    slot_grid = offset_grid * CAP + pair_rank
    send_at = lax.dynamic_slice_in_dim(slot_grid, this_dev, 1, 0)[0]
    buffer_rows = jnp.arange(WINDOW * CAP, dtype=jnp.int32)
    send_table = (buffer_rows[:, None] == send_at[None, :]).astype(BF16)
    arrive_at = slot_grid.reshape(-1)
    slot_match = (owner_dev[None, :] == this_dev) & (state_page[None, :] == positions[:, None])
    pick_from = jnp.sum(jnp.where(slot_match, arrive_at[None, :], 0), axis=1)
    conv_of = jnp.sum(jnp.where(slot_match, conv_page[None, :], 0), axis=1)
    kept_count = jnp.sum(jnp.where(slot_match, accepted[None, :], 0), axis=1)
    gather_table = (buffer_rows[None, :] == pick_from[:, None]).astype(BF16)
    return (send_table, gather_table, conv_of, kept_count)


def tables_kernel(sizes, conv_ref, kept_ref, moves_ref, masks_ref):
    per_dev, draft, hist_pad = sizes
    rows = per_dev * draft
    keep = KCONV - 1
    width = rows + hist_pad

    def pick(slot, scalars):
        return sum(jnp.where(slot == at, scalars[at], 0) for at in range(per_dev))

    row = lax.broadcasted_iota(jnp.int32, (rows, width), 0)
    column = lax.broadcasted_iota(jnp.int32, (rows, width), 1)
    step = row % draft
    page_row = pick(row // draft, conv_ref) * keep
    for delay in range(1, KCONV):
        source = jnp.where(step >= delay, row - delay, rows + page_row + keep + step - delay)
        moves_ref[(delay - 1) * rows : delay * rows, :] = (column == source).astype(F32).astype(BF16)
    out_row = lax.broadcasted_iota(jnp.int32, (hist_pad, width), 0)
    column = lax.broadcasted_iota(jnp.int32, (hist_pad, width), 1)
    out_page, out_at = out_row // keep, out_row % keep
    source = jnp.full((hist_pad, width), -1, jnp.int32)
    for slot in range(per_dev):
        at = kept_ref[slot] + out_at
        held = jnp.where(at < keep, rows + out_page * keep + at, slot * draft + at - keep)
        source = jnp.where(out_page == conv_ref[slot], held, source)
    moves_ref[keep * rows : keep * rows + hist_pad, :] = (column == source).astype(F32).astype(BF16)
    row = lax.broadcasted_iota(jnp.int32, (rows, rows), 0)
    column = lax.broadcasted_iota(jnp.int32, (rows, rows), 1)
    step = row % draft
    kept = pick(row // draft, kept_ref)
    masks_ref[0] = (step < kept).astype(F32)
    masks_ref[1] = (column == row - step + kept - 1).astype(F32)
    same = row // draft == column // draft
    masks_ref[2] = (same & (column <= row)).astype(F32)
    masks_ref[3] = (same & (column >= row)).astype(F32)


def series_tables(conv_of, kept_count, per_dev, draft, hist_pad):
    rows = per_dev * draft
    smem = pl.BlockSpec(memory_space=pltpu.SMEM)
    return pl.pallas_call(
        lambda *refs: tables_kernel((per_dev, draft, hist_pad), *refs),
        in_specs=[smem, smem],
        out_specs=[pl.BlockSpec(memory_space=pltpu.VMEM)] * 2,
        out_shape=[
            jax.ShapeDtypeStruct(((KCONV - 1) * rows + hist_pad, rows + hist_pad), BF16),
            jax.ShapeDtypeStruct((4, rows, rows), F32),
        ],
    )(conv_of, kept_count)


def split_pair(value):
    high = value.astype(BF16)
    return high, (value - high.astype(F32)).astype(BF16)


def convolve(series, current, taps, moves_ref):
    rows = current.shape[0]
    total = taps[KCONV - 1 : KCONV] * current
    for delay in range(1, KCONV):
        move = moves_ref[(delay - 1) * rows : delay * rows, :]
        moved = jnp.dot(move, series, preferred_element_type=F32)
        total = total + taps[KCONV - 1 - delay : KCONV - delay] * moved
    return total / (1.0 + jnp.exp(-total))


def mixer_kernel(sizes, order_ref, *refs):
    chunks, per_dev, draft, heads, head_dim, state_width = sizes
    x_refs, aux_refs, refs = refs[:chunks], refs[chunks : 2 * chunks], refs[2 * chunks :]
    (
        select_ref,
        moves_ref,
        masks_ref,
        hist_ref,
        hist_state_ref,
        taps_ref,
        taps_state_ref,
        skip_ref,
        step_ref,
        state_ref,
        y_ref,
        picked_ref,
        b_ref,
        end_ref,
        conv_ref,
        conv_state_ref,
        c_scr,
        scores_scr,
        log_scr,
        log_t_scr,
        step_t_scr,
        sel_t_scr,
    ) = refs
    rows = per_dev * draft
    width = heads * head_dim
    group = pl.program_id(0)
    edges = moves_ref[(KCONV - 1) * rows :, :]

    @pl.when(group == 0)
    def prepare():
        aux = jnp.dot(aux_refs[0][...], select_ref[0], preferred_element_type=F32)
        for chunk in range(1, chunks):
            aux = aux + jnp.dot(aux_refs[chunk][...], select_ref[chunk], preferred_element_type=F32)
        maps = aux[:, : 2 * state_width]
        series = jnp.concatenate([maps.astype(BF16), hist_state_ref[...]], axis=0)
        active = convolve(series, maps, taps_state_ref[...], moves_ref)
        conv_state_ref[...] = jnp.dot(edges, series, preferred_element_type=F32).astype(BF16)
        b_rows, c_rows = active[:, :state_width], active[:, state_width:]
        c_high, c_low = split_pair(c_rows.T)
        c_scr[:state_width, :rows] = c_high
        c_scr[:state_width, rows:] = c_low
        c_scr[state_width:, :rows] = c_high
        c_scr[state_width:, rows:] = jnp.zeros_like(c_low)
        b_ref[...] = b_rows
        scores_scr[...] = lax.dot_general(
            b_rows, c_rows, (((1,), (1,)), ((), ())), precision=HIGH, preferred_element_type=F32
        ) * masks_ref[3]
        raw = aux[:, 2 * state_width :] + step_ref[:1, :]
        step_size = jnp.maximum(raw, 0.0) + jnp.log1p(jnp.exp(-jnp.abs(raw)))
        log_decay = jnp.dot(
            masks_ref[2], step_size * step_ref[1:2, :], precision=HIGH, preferred_element_type=F32
        )
        end = jnp.dot(masks_ref[1], log_decay, precision=HIGH, preferred_element_type=F32)
        kept = masks_ref[0] > 0.0
        chosen = jnp.where(kept, jnp.exp(jnp.where(kept, end - log_decay, 0.0)), 0.0) * step_size
        end_ref[...] = jnp.exp(end)
        for chunk in range(chunks):
            log_scr[chunk] = log_decay[:, chunk * heads : (chunk + 1) * heads]
        log_t_scr[...] = log_decay.T
        step_t_scr[...] = step_size.T
        sel_t_scr[...] = chosen.T

    x_rows = x_refs[0][...]
    for chunk in range(1, chunks):
        x_rows = jnp.where(order_ref[group] == chunk, x_refs[chunk][...], x_rows)
    series = jnp.concatenate([x_rows, hist_ref[...]], axis=0)
    active = convolve(series, x_rows.astype(F32), taps_ref[...], moves_ref).T
    conv_ref[...] = jnp.dot(edges, series, preferred_element_type=F32).astype(BF16)
    log_here = log_scr[group]
    slot_of = lax.broadcasted_iota(jnp.int32, (width, rows), 1) // draft
    c_all = c_scr[...]
    carried = jnp.zeros((width, rows), F32)
    for slot in range(per_dev):
        high, low = split_pair(state_ref[slot].reshape(width, state_width))
        read = jnp.dot(jnp.concatenate([high, low], axis=1), c_all, preferred_element_type=F32)
        carried = jnp.where(slot_of == slot, read[:, :rows] + read[:, rows:], carried)
    outputs, picked = [], []
    for head in range(heads):
        part = slice(head * head_dim, (head + 1) * head_dim)
        at = group * heads + head
        log_row = log_t_scr[pl.ds(at, 1), :]
        spread = jnp.where(masks_ref[3] > 0.0, log_row - log_here[:, head : head + 1], -1e30)
        weight = (jnp.exp(spread) * scores_scr[...]).astype(BF16)
        x_head = active[part]
        within = jnp.dot(
            (x_head * step_t_scr[pl.ds(at, 1), :]).astype(BF16), weight, preferred_element_type=F32
        )
        outputs.append(within + jnp.exp(log_row) * carried[part] + skip_ref[at] * x_head)
        picked.append(x_head * sel_t_scr[pl.ds(at, 1), :])
    y_ref[...] = jnp.concatenate(outputs, axis=0).T.astype(BF16)
    x_high, x_low = split_pair(jnp.concatenate(picked, axis=0))
    picked_ref[:, :rows] = x_high
    picked_ref[:, rows:] = x_low


def update_kernel(sizes, picked_ref, b_ref, end_ref, state_ref, new_state_ref, b_scr, end_scr):
    steps, per_dev, draft, heads, head_dim, state_width = sizes
    rows = per_dev * draft
    group = pl.program_id(0)

    @pl.when(group == 0)
    def prepare():
        slot = lax.broadcasted_iota(jnp.int32, (rows, state_width), 0) // draft
        for at in range(per_dev):
            high, low = split_pair(jnp.where(slot == at, b_ref[...], 0.0))
            lanes = slice(at * state_width, (at + 1) * state_width)
            b_scr[:rows, lanes] = high
            b_scr[rows : 2 * rows, lanes] = high
            b_scr[2 * rows :, lanes] = low
        for step in range(steps):
            end_scr[step] = end_ref[:, step * heads : (step + 1) * heads]

    end_here = end_scr[group]
    picked = jnp.concatenate([picked_ref[...], picked_ref[:, :rows]], axis=1)
    for pair in range(0, per_dev, 2):
        update = jnp.dot(
            picked,
            b_scr[:, pair * state_width : (pair + 2) * state_width],
            preferred_element_type=F32,
        )
        for slot in range(pair, pair + 2):
            lanes = slice((slot - pair) * state_width, (slot - pair + 1) * state_width)
            for head in range(heads):
                part = slice(head * head_dim, (head + 1) * head_dim)
                keep = end_here[slot * draft : slot * draft + 1, head : head + 1]
                new_state_ref[slot, head] = keep * state_ref[slot, head] + update[part, lanes]


def update_states(picked, b_rows, ends, state_pool):
    per_dev, all_heads, head_dim, state_width = state_pool.shape
    rows = b_rows.shape[0]
    steps = 4
    heads = all_heads // steps
    sizes = (steps, per_dev, rows // per_dev, heads, head_dim, state_width)
    state_spec = pl.BlockSpec((per_dev, heads, head_dim, state_width), lambda group: (0, group, 0, 0))
    return pl.pallas_call(
        lambda *refs: update_kernel(sizes, *refs),
        grid=(steps,),
        in_specs=[
            pl.BlockSpec((heads * head_dim, 2 * rows), lambda group: (group, 0)),
            pl.BlockSpec(b_rows.shape, lambda group: (0, 0)),
            pl.BlockSpec(ends.shape, lambda group: (0, 0)),
            state_spec,
        ],
        out_specs=state_spec,
        scratch_shapes=[
            pltpu.VMEM((3 * rows, per_dev * state_width), BF16),
            pltpu.VMEM((steps, rows, heads), F32),
        ],
        out_shape=jax.ShapeDtypeStruct(state_pool.shape, F32),
        compiler_params=pltpu.CompilerParams(vmem_limit_bytes=VMEM_LIMIT),
        cost_estimate=pl.CostEstimate(
            flops=64 * rows * rows * all_heads * head_dim,
            bytes_accessed=8 * state_pool.size,
            transcendentals=0,
        ),
    )(picked, b_rows, ends, state_pool)


def mix_requests(
    packed,
    order,
    select,
    tables,
    history,
    history_state,
    taps,
    taps_state,
    skip_gain,
    steps,
    state_pool,
):
    rows, packed_width = packed[0].shape
    chunks = len(packed)
    per_dev, all_heads, head_dim, state_width = state_pool.shape
    hist_pad, inner = history.shape
    heads = all_heads // chunks
    draft = rows // per_dev
    lanes = inner // chunks
    aux_lanes = packed_width - lanes
    moves, masks = tables
    sizes = (chunks, per_dev, draft, heads, head_dim, state_width)

    def whole(array):
        zeros = (0,) * array.ndim
        return pl.BlockSpec(array.shape, lambda group, order_ref: zeros)

    def by_group(height):
        return pl.BlockSpec((height, lanes), lambda group, order_ref: (0, group))

    x_spec = pl.BlockSpec((rows, lanes), lambda group, order_ref: (0, 0))
    aux_spec = pl.BlockSpec(
        (rows, aux_lanes), lambda group, order_ref: (0, lanes // aux_lanes)
    )

    state_spec = pl.BlockSpec(
        (per_dev, heads, head_dim, state_width), lambda group, order_ref: (0, group, 0, 0)
    )
    step_lanes = select.shape[2] - 2 * state_width
    grid_spec = pltpu.PrefetchScalarGridSpec(
        num_scalar_prefetch=1,
        grid=(chunks,),
        in_specs=[
            *[x_spec] * chunks,
            *[aux_spec] * chunks,
            whole(select),
            whole(moves),
            whole(masks),
            by_group(hist_pad),
            whole(history_state),
            by_group(KCONV),
            whole(taps_state),
            pl.BlockSpec(memory_space=pltpu.SMEM),
            whole(steps),
            state_spec,
        ],
        out_specs=[
            by_group(rows),
            pl.BlockSpec((heads * head_dim, 2 * rows), lambda group, order_ref: (group, 0)),
            pl.BlockSpec((rows, state_width), lambda group, order_ref: (0, 0)),
            pl.BlockSpec((rows, step_lanes), lambda group, order_ref: (0, 0)),
            by_group(hist_pad),
            pl.BlockSpec((hist_pad, 2 * state_width), lambda group, order_ref: (0, 0)),
        ],
        scratch_shapes=[
            pltpu.VMEM((2 * state_width, 2 * rows), BF16),
            pltpu.VMEM((rows, rows), F32),
            pltpu.VMEM((chunks, rows, heads), F32),
            pltpu.VMEM((step_lanes, rows), F32),
            pltpu.VMEM((step_lanes, rows), F32),
            pltpu.VMEM((step_lanes, rows), F32),
        ],
    )
    return pl.pallas_call(
        lambda *refs: mixer_kernel(sizes, *refs),
        grid_spec=grid_spec,
        out_shape=(
            jax.ShapeDtypeStruct((rows, inner), BF16),
            jax.ShapeDtypeStruct((inner, 2 * rows), BF16),
            jax.ShapeDtypeStruct((rows, state_width), F32),
            jax.ShapeDtypeStruct((rows, step_lanes), F32),
            jax.ShapeDtypeStruct((hist_pad, inner), BF16),
            jax.ShapeDtypeStruct((hist_pad, 2 * state_width), BF16),
        ),
        compiler_params=pltpu.CompilerParams(vmem_limit_bytes=VMEM_LIMIT),
        cost_estimate=pl.CostEstimate(
            flops=64 * rows * rows * all_heads * head_dim,
            bytes_accessed=8 * state_pool.size,
            transcendentals=rows * rows * all_heads,
        ),
    )(
        order,
        *packed,
        *packed,
        select,
        moves,
        masks,
        history,
        history_state,
        taps,
        taps_state,
        skip_gain,
        steps,
        state_pool,
    )


def by_chunk(array, chunks, lanes):
    rows, width = array.shape
    parts = array.reshape(rows, chunks, width // chunks).transpose(1, 0, 2)
    return jnp.pad(parts, ((0, 0), (0, 0), (0, lanes - width // chunks)))


def swap(value, axis):
    return rotate(value, axis, 1)


def near_half(weight):
    me = lax.axis_index("near")
    keep = lax.dynamic_index_in_dim(weight, me, 0, keepdims=False)
    give = lax.dynamic_index_in_dim(weight, 1 - me, 0, keepdims=False)
    take = swap(give, "near")
    return jnp.concatenate([jnp.where(me == 0, keep, take), jnp.where(me == 0, take, keep)])


def tie(value, *others):
    return lax.optimization_barrier((value,) + others)[0]


def out_kernel(place_ref, own_ref, peer_ref, *refs):
    weight_refs, own_out_ref, both_out_ref = refs[:8], refs[8], refs[9]
    rows = own_ref.shape[0]
    both = jnp.concatenate([own_ref[...], peer_ref[...]], axis=0)
    for pair in range(4):
        weight = jnp.concatenate([weight_refs[2 * pair][...], weight_refs[2 * pair + 1][...]], axis=1)
        total = jnp.dot(both, weight, preferred_element_type=F32)
        for at in range(2):
            start = place_ref[(2 * pair + at) % 4] * LANES
            lanes = pl.ds(pl.multiple_of(start, LANES), LANES)
            columns = slice(at * LANES, (at + 1) * LANES)
            own_out_ref[pair // 2, :, lanes] = total[:rows, columns]
            for group in range(2):
                part = total[group * rows : (group + 1) * rows, columns]
                both_out_ref[pair // 2, group, :, lanes] = part.astype(BF16)


def project_out(own, peer, weights, place_of):
    rows, depth = own.shape
    whole = pl.BlockSpec(memory_space=pltpu.VMEM)
    return pl.pallas_call(
        out_kernel,
        in_specs=[pl.BlockSpec(memory_space=pltpu.SMEM)] + [whole] * 10,
        out_specs=[whole, whole],
        out_shape=[
            jax.ShapeDtypeStruct((2, rows, 4 * LANES), F32),
            jax.ShapeDtypeStruct((2, 2, rows, 4 * LANES), BF16),
        ],
        compiler_params=pltpu.CompilerParams(vmem_limit_bytes=24 * 1024 * 1024),
        cost_estimate=QUICK,
    )(place_of, own, peer, *weights)


def on_device(
    hidden_in,
    z_weight,
    x_weight,
    state_proj,
    step_weight,
    step_bias,
    decay_log,
    skip_gain,
    conv_inner,
    conv_state,
    norm_gain,
    out_weight,
    state_pool,
    conv_pool_inner,
    conv_pool_state,
    owner_dev,
    state_page,
    conv_page,
    accepted,
):
    groups = lax.axis_size(RING)
    fars, nears, sides, cores = (lax.axis_size(name) for name in RING)
    splits = lax.axis_size("mdl")
    paired = (fars, nears, sides, cores, splits) == (2, 2, 2, 2, 2)
    paired = paired and hidden_in.shape[1] == groups * LANES
    chunks = fars * nears if paired else nears
    this_dev = lax.axis_index(RING)
    near_at = lax.axis_index("near")
    me = lax.axis_index(SLABS) if paired else near_at
    part = lax.axis_index("mdl")
    per_dev, all_heads, head_dim, state_width = state_pool.shape
    rows, depth = hidden_in.shape
    draft = rows // per_dev
    inner = all_heads * head_dim
    slots = WINDOW * CAP
    chunk_width = inner // chunks
    lanes = chunk_width
    map_width = 2 * state_width // chunks
    heads = all_heads // chunks
    aux_lanes = round_up(map_width + heads, LANES)
    keep = KCONV - 1
    hist_rows = per_dev * keep
    hist_pad = round_up(hist_rows, 32)

    send_table, gather_table, conv_of, kept_count = route_tables(
        owner_dev, state_page, conv_page, accepted, groups, per_dev, this_dev
    )

    block = depth // groups
    columns = hidden_in.reshape(rows, fars, nears, sides, cores, block).transpose(0, 4, 3, 1, 2, 5)
    columns = columns.reshape(rows, splits, depth // splits)
    share = lax.dynamic_index_in_dim(columns, part, 1, keepdims=False)
    outgoing = one_hot_apply(send_table, share, (slots, draft, depth // splits))

    def prepare(after):
        conv_now, kept_now, pool_inner, pool_state, bias, rate = lax.optimization_barrier(
            (conv_of, kept_count, conv_pool_inner, conv_pool_state, step_bias, decay_log, after)
        )[:6]
        order = (jnp.arange(chunks, dtype=jnp.int32) - me) % chunks
        home_chunk = (jnp.arange(chunks, dtype=jnp.int32) + me) % chunks
        lane = jnp.arange(aux_lanes, dtype=jnp.int32)[None, :]
        step_lanes = round_up(all_heads, LANES)
        target = jnp.where(
            lane < map_width,
            home_chunk[:, None] * map_width + lane,
            jnp.where(
                lane < map_width + heads,
                2 * state_width + home_chunk[:, None] * heads + lane - map_width,
                -1,
            ),
        )
        select = (
            target[:, :, None] == jnp.arange(2 * state_width + step_lanes, dtype=jnp.int32)
        ).astype(BF16)
        tables = series_tables(conv_now, kept_now, per_dev, draft, hist_pad)
        pad_rows = ((0, hist_pad - hist_rows), (0, 0))
        history = jnp.pad(pool_inner.reshape(hist_rows, inner), pad_rows)
        history_state = jnp.pad(pool_state.reshape(hist_rows, 2 * state_width), pad_rows)
        pad_heads = ((0, 0), (0, step_lanes - all_heads))
        steps = jnp.pad(jnp.stack([bias, -jnp.exp(rate)]), pad_heads)
        return order, select, tables, history, history_state, steps

    def route(slots_out):
        return [
            rotate(slots_out[offset * CAP : (offset + 1) * CAP], RING, offset)
            for offset in range(WINDOW)
        ]

    packed_weight = jnp.concatenate(
        [
            by_chunk(x_weight, chunks, lanes),
            by_chunk(state_proj, chunks, map_width),
            by_chunk(step_weight, chunks, aux_lanes - map_width),
            by_chunk(z_weight, chunks, lanes),
        ],
        axis=2,
    )
    split = lanes + aux_lanes
    width = split + lanes
    far, side, core = (lax.axis_index(name) for name in ("far", "side", "core"))
    if paired:
        incoming = route(outgoing)
        packed_weight, early = lax.optimization_barrier((packed_weight, incoming[: WINDOW - 2]))
        pieces = [
            rotate(
                lax.dynamic_index_in_dim(packed_weight, (me + step) % chunks, 0, keepdims=False),
                SLABS,
                step,
            )
            for step in range(chunks)
        ]
        side_own = swap(pieces[0], "side")
        extras = prepare(early)
        incoming, pieces, side_own, extras = lax.optimization_barrier(
            (early + incoming[WINDOW - 2 :], pieces, side_own, extras)
        )
        owned = one_hot_apply(gather_table, jnp.concatenate(incoming), (rows, depth // splits))
        owned, pieces = lax.optimization_barrier((owned, pieces))
        rows_of = [rotate(owned, SLABS, step) for step in range(chunks)]
        slabs = [(me - step) % chunks for step in range(chunks)]
        across = swap(jnp.stack(pieces[1:]), "side")
        held = place(pieces, slabs)
        rows_of, across, held = lax.optimization_barrier((rows_of, across, held))
        across = place([side_own] + [across[at] for at in range(chunks - 1)], slabs)
        own_rows = jnp.concatenate(rows_of)
        peer_rows = swap(own_rows, "mdl")
        at_core, at_side, at_half = core == 0, side == 0, part == 0
        held_peer, across_peer = swap(held, "core"), swap(across, "core")

        def full(columns):
            own = [value[:, :, columns].reshape(-1, columns.stop - columns.start) for value in (held, across)]
            peer = [
                value[:, :, columns].reshape(-1, columns.stop - columns.start)
                for value in (held_peer, across_peer)
            ]
            parts = []
            for first, second in ((own, peer), (peer, own)):
                low = [jnp.where(at_core, first[at], second[at]) for at in range(2)]
                parts += [jnp.where(at_side, low[0], low[1]), jnp.where(at_side, low[1], low[0])]
            return jnp.concatenate(parts)

        packed_full, gate_full = full(slice(0, split)), full(slice(split, width))
        out_far, out_side = swap(out_weight, "far"), swap(out_weight, "side")
        own_rows, peer_rows, packed_full, gate_full, out_far, out_side = lax.optimization_barrier(
            (own_rows, peer_rows, packed_full, gate_full, out_far, out_side)
        )
        all_rows = jnp.concatenate(
            [jnp.where(at_half, own_rows, peer_rows), jnp.where(at_half, peer_rows, own_rows)], axis=1
        )
        packed = jnp.dot(all_rows, packed_full, preferred_element_type=F32).astype(BF16)
        packed = packed.reshape(chunks, rows, split)
        packed = [rotate(packed[step], SLABS, -step) for step in range(chunks)]
        gate = jnp.dot(all_rows, gate_full, preferred_element_type=F32).astype(BF16)
        gate = gate.reshape(chunks, rows, lanes)
        out_across = swap(out_far, "side")
        packed, gate, out_across = lax.optimization_barrier((packed, gate, out_across))
        gate = [rotate(gate[step], SLABS, -step) for step in range(chunks)]
        out_columns = []
        for column in (out_weight, out_side, out_far, out_across):
            out_columns += [column, swap(column, "core")]
    else:
        incoming = route(outgoing)
        extras = prepare(outgoing)
        owned = one_hot_apply(gather_table, jnp.concatenate(incoming), (rows, depth // splits))
        owned = lax.all_gather(owned, "mdl", axis=1, tiled=True)
        owned = jnp.concatenate([owned, swap(owned, "near")])
        weight = near_half(packed_weight)
        for name in ("far", "side", "core"):
            weight = lax.all_gather(weight, name, axis=0, tiled=True)
        total = jnp.dot(owned, weight, preferred_element_type=F32).astype(BF16)
        total = [total[:rows], swap(total[rows:], "near")]
        packed = [value[:, :split] for value in total]
        gate = [value[:, split:] for value in total]
        out_columns = lax.all_gather(out_weight, RING, axis=1, tiled=True)

    order, select, tables, history, history_state, steps = extras
    y_rows, picked, b_rows, ends, conv_rows, conv_state_rows = mix_requests(
        packed,
        order,
        select,
        tables,
        history,
        history_state,
        conv_inner,
        conv_state,
        skip_gain,
        steps,
        state_pool,
    )

    gate_here = []
    for chunk in range(chunks):
        value = gate[0]
        for step in range(1, chunks):
            value = jnp.where(me == (chunk - step) % chunks, gate[step], value)
        gate_here.append(value)
    gate_here = jnp.concatenate(gate_here, axis=1).astype(F32)
    gated = y_rows.astype(F32) * (gate_here / (1.0 + jnp.exp(-gate_here)))
    squares = jnp.sum(gated * gated, axis=1)
    scaled = (gated * norm_gain).astype(BF16)
    new_states = update_states(picked, tie(b_rows, scaled), ends, state_pool)
    wide = depth // splits
    total_inner = inner * splits
    if paired:
        squares = squares + swap(squares, "mdl")
        scale = lax.rsqrt(squares / total_inner + EPSILON)
        columns_at = jnp.stack(
            [2 * at_side + at_core for at_side in (side, 1 - side) for at_core in (core, 1 - core)]
        )
        terms, given = project_out(scaled, tie(swap(scaled, "near"), new_states), out_columns, columns_at)
        here = far == part
        mine = jnp.where(here, terms[0], terms[1])
        other = jnp.where(here, given[1, 0], given[0, 0])
        peer_mine = jnp.where(here, given[0, 1], given[1, 1])
        peer_other = jnp.where(here, given[1, 1], given[0, 1])
        over_y = swap(other, "mdl")
        over_near = swap(peer_mine, "near")
        over_both = lax.ppermute(peer_other, ("near", "mdl"), [(0, 3), (1, 2), (2, 1), (3, 0)])
        here = (mine + over_y.astype(F32)) * scale[:, None]
        there = (over_near.astype(F32) + over_both.astype(F32)) * scale[:, None]
        here, there = here.astype(BF16), there.astype(BF16)
        mixed_rows = jnp.concatenate(
            [jnp.where(near_at == 0, here, there), jnp.where(near_at == 0, there, here)], axis=1
        )
    else:
        terms = jnp.dot(scaled, out_columns, preferred_element_type=F32)
        squares = lax.psum(squares, "mdl")
        total = lax.psum_scatter(terms, "mdl", scatter_dimension=1, tiled=True)
        scale = lax.rsqrt(squares / total_inner + EPSILON)
        mixed_rows = (total * scale[:, None]).astype(BF16)

    returning = one_hot_apply(
        gather_table.T, mixed_rows.reshape(per_dev, draft, wide), (slots, draft, wide)
    )
    arrived = jnp.concatenate(
        [
            rotate(returning[offset * CAP : (offset + 1) * CAP], RING, -offset)
            for offset in range(WINDOW)
        ],
        axis=0,
    )
    mixed = one_hot_apply(send_table.T, arrived, (rows, wide))
    return (
        mixed,
        new_states,
        conv_rows[:hist_rows].reshape(per_dev, keep, inner),
        conv_state_rows[:hist_rows].reshape(per_dev, keep, 2 * state_width),
    )


def solution(mesh):
    sizes = factor(mesh.shape["req"])
    split_mesh = Mesh(mesh.devices.reshape(*sizes, mesh.shape["mdl"]), RING + ("mdl",))
    return jax.shard_map(
        on_device,
        mesh=split_mesh,
        in_specs=(
            P(RING, None),
            P(RING, "mdl"),
            P(RING, "mdl"),
            P(RING, None),
            P(RING, "mdl"),
            P("mdl"),
            P("mdl"),
            P("mdl"),
            P(None, "mdl"),
            P(),
            P("mdl"),
            P("mdl", RING),
            P(RING, "mdl", None, None),
            P(RING, None, "mdl"),
            P(RING, None, None),
            P(),
            P(),
            P(),
            P(),
        ),
        out_specs=(
            P(RING, "mdl"),
            P(RING, "mdl", None, None),
            P(RING, None, "mdl"),
            P(RING, None, None),
        ),
        check_vma=False,
    )
```

```python
import jax
import jax.numpy as jnp
from jax import lax
from jax.experimental import pallas as pl
from jax.experimental.pallas import tpu as pltpu
from jax.sharding import Mesh, PartitionSpec as P

KCONV = 4
CAP = 2
WINDOW = 8
LANES = 128
QUICK = pl.CostEstimate(flops=1000, bytes_accessed=1000, transcendentals=0)
VMEM_LIMIT = 56 * 1024 * 1024
EPSILON = 1e-05
HIGH = lax.Precision.HIGHEST
BF16 = jnp.bfloat16
F32 = jnp.float32

RING = ("far", "near", "side", "core")
SLABS = ("far", "near")


def round_up(value, unit):
    return -(-value // unit) * unit


def factor(count):
    core, near = 2, 2
    chips = count // core
    side = 1
    while (2 * side) ** 2 <= chips:
        side *= 2
    return chips // side // near, near, side, core


def rotate(value, axis, steps):
    count = lax.axis_size(axis)
    if steps % count == 0:
        return value
    pairs = [(source, (source + steps) % count) for source in range(count)]
    return lax.ppermute(value, axis, pairs)


def gather_axis(value, axis, dim):
    count = lax.axis_size(axis)
    if count == 1:
        return value
    if count > 2:
        return lax.all_gather(value, axis, axis=dim, tiled=True)
    peer = rotate(value, axis, 1)
    first = lax.axis_index(axis) == 0
    return jnp.concatenate(
        [jnp.where(first, value, peer), jnp.where(first, peer, value)], axis=dim
    )


def place(pieces, slots):
    full = jnp.zeros((len(pieces),) + pieces[0].shape, pieces[0].dtype)
    for piece, slot in zip(pieces, slots):
        full = lax.dynamic_update_slice_in_dim(full, piece[None], slot, 0)
    return full


def one_hot_apply(table, values, shape):
    flat = values.reshape(table.shape[1], -1)
    return jnp.dot(table, flat, preferred_element_type=F32).astype(BF16).reshape(shape)


def route_tables(owner_dev, state_page, conv_page, accepted, groups, per_dev, this_dev):
    owner_grid = owner_dev.reshape(groups, per_dev)
    home_grid = jnp.arange(groups, dtype=jnp.int32)[:, None]
    offset_grid = (owner_grid - home_grid + groups) % groups
    positions = jnp.arange(per_dev, dtype=jnp.int32)
    earlier = positions[None, :] < positions[:, None]
    pair_rank = jnp.sum((owner_grid[:, :, None] == owner_grid[:, None, :]) & earlier[None], axis=2)
    slot_grid = offset_grid * CAP + pair_rank
    send_at = lax.dynamic_slice_in_dim(slot_grid, this_dev, 1, 0)[0]
    buffer_rows = jnp.arange(WINDOW * CAP, dtype=jnp.int32)
    send_table = (buffer_rows[:, None] == send_at[None, :]).astype(BF16)
    arrive_at = slot_grid.reshape(-1)
    slot_match = (owner_dev[None, :] == this_dev) & (state_page[None, :] == positions[:, None])
    pick_from = jnp.sum(jnp.where(slot_match, arrive_at[None, :], 0), axis=1)
    conv_of = jnp.sum(jnp.where(slot_match, conv_page[None, :], 0), axis=1)
    kept_count = jnp.sum(jnp.where(slot_match, accepted[None, :], 0), axis=1)
    gather_table = (buffer_rows[None, :] == pick_from[:, None]).astype(BF16)
    return (send_table, gather_table, conv_of, kept_count)


def tables_kernel(sizes, conv_ref, kept_ref, moves_ref, masks_ref):
    per_dev, draft, hist_pad = sizes
    rows = per_dev * draft
    keep = KCONV - 1
    width = rows + hist_pad

    def pick(slot, scalars):
        return sum(jnp.where(slot == at, scalars[at], 0) for at in range(per_dev))

    row = lax.broadcasted_iota(jnp.int32, (rows, width), 0)
    column = lax.broadcasted_iota(jnp.int32, (rows, width), 1)
    step = row % draft
    page_row = pick(row // draft, conv_ref) * keep
    for delay in range(1, KCONV):
        source = jnp.where(step >= delay, row - delay, rows + page_row + keep + step - delay)
        moves_ref[(delay - 1) * rows : delay * rows, :] = (column == source).astype(F32).astype(BF16)
    out_row = lax.broadcasted_iota(jnp.int32, (hist_pad, width), 0)
    column = lax.broadcasted_iota(jnp.int32, (hist_pad, width), 1)
    out_page, out_at = out_row // keep, out_row % keep
    source = jnp.full((hist_pad, width), -1, jnp.int32)
    for slot in range(per_dev):
        at = kept_ref[slot] + out_at
        held = jnp.where(at < keep, rows + out_page * keep + at, slot * draft + at - keep)
        source = jnp.where(out_page == conv_ref[slot], held, source)
    moves_ref[keep * rows : keep * rows + hist_pad, :] = (column == source).astype(F32).astype(BF16)
    row = lax.broadcasted_iota(jnp.int32, (rows, rows), 0)
    column = lax.broadcasted_iota(jnp.int32, (rows, rows), 1)
    step = row % draft
    kept = pick(row // draft, kept_ref)
    masks_ref[0] = (step < kept).astype(F32)
    masks_ref[1] = (column == row - step + kept - 1).astype(F32)
    same = row // draft == column // draft
    masks_ref[2] = (same & (column <= row)).astype(F32)
    masks_ref[3] = (same & (column >= row)).astype(F32)


def series_tables(conv_of, kept_count, per_dev, draft, hist_pad):
    rows = per_dev * draft
    smem = pl.BlockSpec(memory_space=pltpu.SMEM)
    return pl.pallas_call(
        lambda *refs: tables_kernel((per_dev, draft, hist_pad), *refs),
        in_specs=[smem, smem],
        out_specs=[pl.BlockSpec(memory_space=pltpu.VMEM)] * 2,
        out_shape=[
            jax.ShapeDtypeStruct(((KCONV - 1) * rows + hist_pad, rows + hist_pad), BF16),
            jax.ShapeDtypeStruct((4, rows, rows), F32),
        ],
    )(conv_of, kept_count)


def split_pair(value):
    high = value.astype(BF16)
    return high, (value - high.astype(F32)).astype(BF16)


def convolve(series, current, taps, moves_ref):
    rows = current.shape[0]
    total = taps[KCONV - 1 : KCONV] * current
    for delay in range(1, KCONV):
        move = moves_ref[(delay - 1) * rows : delay * rows, :]
        moved = jnp.dot(move, series, preferred_element_type=F32)
        total = total + taps[KCONV - 1 - delay : KCONV - delay] * moved
    return total / (1.0 + jnp.exp(-total))


def mixer_kernel(sizes, order_ref, *refs):
    chunks, per_dev, draft, heads, head_dim, state_width = sizes
    x_refs, aux_refs, refs = refs[:chunks], refs[chunks : 2 * chunks], refs[2 * chunks :]
    (
        select_ref,
        moves_ref,
        masks_ref,
        hist_ref,
        hist_state_ref,
        taps_ref,
        taps_state_ref,
        skip_ref,
        step_ref,
        state_ref,
        y_ref,
        picked_ref,
        b_ref,
        end_ref,
        conv_ref,
        conv_state_ref,
        c_scr,
        scores_scr,
        log_scr,
        log_t_scr,
        step_t_scr,
        sel_t_scr,
    ) = refs
    rows = per_dev * draft
    width = heads * head_dim
    group = pl.program_id(0)
    edges = moves_ref[(KCONV - 1) * rows :, :]

    @pl.when(group == 0)
    def prepare():
        aux = jnp.dot(aux_refs[0][...], select_ref[0], preferred_element_type=F32)
        for chunk in range(1, chunks):
            aux = aux + jnp.dot(aux_refs[chunk][...], select_ref[chunk], preferred_element_type=F32)
        maps = aux[:, : 2 * state_width]
        series = jnp.concatenate([maps.astype(BF16), hist_state_ref[...]], axis=0)
        active = convolve(series, maps, taps_state_ref[...], moves_ref)
        conv_state_ref[...] = jnp.dot(edges, series, preferred_element_type=F32).astype(BF16)
        b_rows, c_rows = active[:, :state_width], active[:, state_width:]
        c_high, c_low = split_pair(c_rows.T)
        c_scr[:state_width, :rows] = c_high
        c_scr[:state_width, rows:] = c_low
        c_scr[state_width:, :rows] = c_high
        c_scr[state_width:, rows:] = jnp.zeros_like(c_low)
        b_ref[...] = b_rows
        scores_scr[...] = lax.dot_general(
            b_rows, c_rows, (((1,), (1,)), ((), ())), precision=HIGH, preferred_element_type=F32
        ) * masks_ref[3]
        raw = aux[:, 2 * state_width :] + step_ref[:1, :]
        step_size = jnp.maximum(raw, 0.0) + jnp.log1p(jnp.exp(-jnp.abs(raw)))
        log_decay = jnp.dot(
            masks_ref[2], step_size * step_ref[1:2, :], precision=HIGH, preferred_element_type=F32
        )
        end = jnp.dot(masks_ref[1], log_decay, precision=HIGH, preferred_element_type=F32)
        kept = masks_ref[0] > 0.0
        chosen = jnp.where(kept, jnp.exp(jnp.where(kept, end - log_decay, 0.0)), 0.0) * step_size
        end_ref[...] = jnp.exp(end)
        for chunk in range(chunks):
            log_scr[chunk] = log_decay[:, chunk * heads : (chunk + 1) * heads]
        log_t_scr[...] = log_decay.T
        step_t_scr[...] = step_size.T
        sel_t_scr[...] = chosen.T

    x_rows = x_refs[0][...]
    for chunk in range(1, chunks):
        x_rows = jnp.where(order_ref[group] == chunk, x_refs[chunk][...], x_rows)
    series = jnp.concatenate([x_rows, hist_ref[...]], axis=0)
    active = convolve(series, x_rows.astype(F32), taps_ref[...], moves_ref).T
    conv_ref[...] = jnp.dot(edges, series, preferred_element_type=F32).astype(BF16)
    log_here = log_scr[group]
    slot_of = lax.broadcasted_iota(jnp.int32, (width, rows), 1) // draft
    c_all = c_scr[...]
    carried = jnp.zeros((width, rows), F32)
    for slot in range(per_dev):
        high, low = split_pair(state_ref[slot].reshape(width, state_width))
        read = jnp.dot(jnp.concatenate([high, low], axis=1), c_all, preferred_element_type=F32)
        carried = jnp.where(slot_of == slot, read[:, :rows] + read[:, rows:], carried)
    outputs, picked = [], []
    for head in range(heads):
        part = slice(head * head_dim, (head + 1) * head_dim)
        at = group * heads + head
        log_row = log_t_scr[pl.ds(at, 1), :]
        spread = jnp.where(masks_ref[3] > 0.0, log_row - log_here[:, head : head + 1], -1e30)
        weight = (jnp.exp(spread) * scores_scr[...]).astype(BF16)
        x_head = active[part]
        within = jnp.dot(
            (x_head * step_t_scr[pl.ds(at, 1), :]).astype(BF16), weight, preferred_element_type=F32
        )
        outputs.append(within + jnp.exp(log_row) * carried[part] + skip_ref[at] * x_head)
        picked.append(x_head * sel_t_scr[pl.ds(at, 1), :])
    y_ref[...] = jnp.concatenate(outputs, axis=0).T.astype(BF16)
    x_high, x_low = split_pair(jnp.concatenate(picked, axis=0))
    picked_ref[:, :rows] = x_high
    picked_ref[:, rows:] = x_low


def update_kernel(sizes, picked_ref, b_ref, end_ref, state_ref, new_state_ref, b_scr, end_scr):
    steps, per_dev, draft, heads, head_dim, state_width = sizes
    rows = per_dev * draft
    group = pl.program_id(0)

    @pl.when(group == 0)
    def prepare():
        slot = lax.broadcasted_iota(jnp.int32, (rows, state_width), 0) // draft
        for at in range(per_dev):
            high, low = split_pair(jnp.where(slot == at, b_ref[...], 0.0))
            lanes = slice(at * state_width, (at + 1) * state_width)
            b_scr[:rows, lanes] = high
            b_scr[rows : 2 * rows, lanes] = high
            b_scr[2 * rows :, lanes] = low
        for step in range(steps):
            end_scr[step] = end_ref[:, step * heads : (step + 1) * heads]

    end_here = end_scr[group]
    picked = jnp.concatenate([picked_ref[...], picked_ref[:, :rows]], axis=1)
    for pair in range(0, per_dev, 2):
        update = jnp.dot(
            picked,
            b_scr[:, pair * state_width : (pair + 2) * state_width],
            preferred_element_type=F32,
        )
        for slot in range(pair, pair + 2):
            lanes = slice((slot - pair) * state_width, (slot - pair + 1) * state_width)
            for head in range(heads):
                part = slice(head * head_dim, (head + 1) * head_dim)
                keep = end_here[slot * draft : slot * draft + 1, head : head + 1]
                new_state_ref[slot, head] = keep * state_ref[slot, head] + update[part, lanes]


def update_states(picked, b_rows, ends, state_pool):
    per_dev, all_heads, head_dim, state_width = state_pool.shape
    rows = b_rows.shape[0]
    steps = 4
    heads = all_heads // steps
    sizes = (steps, per_dev, rows // per_dev, heads, head_dim, state_width)
    state_spec = pl.BlockSpec((per_dev, heads, head_dim, state_width), lambda group: (0, group, 0, 0))
    return pl.pallas_call(
        lambda *refs: update_kernel(sizes, *refs),
        grid=(steps,),
        in_specs=[
            pl.BlockSpec((heads * head_dim, 2 * rows), lambda group: (group, 0)),
            pl.BlockSpec(b_rows.shape, lambda group: (0, 0)),
            pl.BlockSpec(ends.shape, lambda group: (0, 0)),
            state_spec,
        ],
        out_specs=state_spec,
        scratch_shapes=[
            pltpu.VMEM((3 * rows, per_dev * state_width), BF16),
            pltpu.VMEM((steps, rows, heads), F32),
        ],
        out_shape=jax.ShapeDtypeStruct(state_pool.shape, F32),
        compiler_params=pltpu.CompilerParams(vmem_limit_bytes=VMEM_LIMIT),
        cost_estimate=pl.CostEstimate(
            flops=64 * rows * rows * all_heads * head_dim,
            bytes_accessed=8 * state_pool.size,
            transcendentals=0,
        ),
    )(picked, b_rows, ends, state_pool)


def mix_requests(
    packed,
    order,
    select,
    tables,
    history,
    history_state,
    taps,
    taps_state,
    skip_gain,
    steps,
    state_pool,
):
    rows, packed_width = packed[0].shape
    chunks = len(packed)
    per_dev, all_heads, head_dim, state_width = state_pool.shape
    hist_pad, inner = history.shape
    heads = all_heads // chunks
    draft = rows // per_dev
    lanes = inner // chunks
    aux_lanes = packed_width - lanes
    moves, masks = tables
    sizes = (chunks, per_dev, draft, heads, head_dim, state_width)

    def whole(array):
        zeros = (0,) * array.ndim
        return pl.BlockSpec(array.shape, lambda group, order_ref: zeros)

    def by_group(height):
        return pl.BlockSpec((height, lanes), lambda group, order_ref: (0, group))

    x_spec = pl.BlockSpec((rows, lanes), lambda group, order_ref: (0, 0))
    aux_spec = pl.BlockSpec(
        (rows, aux_lanes), lambda group, order_ref: (0, lanes // aux_lanes)
    )

    state_spec = pl.BlockSpec(
        (per_dev, heads, head_dim, state_width), lambda group, order_ref: (0, group, 0, 0)
    )
    step_lanes = select.shape[2] - 2 * state_width
    grid_spec = pltpu.PrefetchScalarGridSpec(
        num_scalar_prefetch=1,
        grid=(chunks,),
        in_specs=[
            *[x_spec] * chunks,
            *[aux_spec] * chunks,
            whole(select),
            whole(moves),
            whole(masks),
            by_group(hist_pad),
            whole(history_state),
            by_group(KCONV),
            whole(taps_state),
            pl.BlockSpec(memory_space=pltpu.SMEM),
            whole(steps),
            state_spec,
        ],
        out_specs=[
            by_group(rows),
            pl.BlockSpec((heads * head_dim, 2 * rows), lambda group, order_ref: (group, 0)),
            pl.BlockSpec((rows, state_width), lambda group, order_ref: (0, 0)),
            pl.BlockSpec((rows, step_lanes), lambda group, order_ref: (0, 0)),
            by_group(hist_pad),
            pl.BlockSpec((hist_pad, 2 * state_width), lambda group, order_ref: (0, 0)),
        ],
        scratch_shapes=[
            pltpu.VMEM((2 * state_width, 2 * rows), BF16),
            pltpu.VMEM((rows, rows), F32),
            pltpu.VMEM((chunks, rows, heads), F32),
            pltpu.VMEM((step_lanes, rows), F32),
            pltpu.VMEM((step_lanes, rows), F32),
            pltpu.VMEM((step_lanes, rows), F32),
        ],
    )
    return pl.pallas_call(
        lambda *refs: mixer_kernel(sizes, *refs),
        grid_spec=grid_spec,
        out_shape=(
            jax.ShapeDtypeStruct((rows, inner), BF16),
            jax.ShapeDtypeStruct((inner, 2 * rows), BF16),
            jax.ShapeDtypeStruct((rows, state_width), F32),
            jax.ShapeDtypeStruct((rows, step_lanes), F32),
            jax.ShapeDtypeStruct((hist_pad, inner), BF16),
            jax.ShapeDtypeStruct((hist_pad, 2 * state_width), BF16),
        ),
        compiler_params=pltpu.CompilerParams(vmem_limit_bytes=VMEM_LIMIT),
        cost_estimate=pl.CostEstimate(
            flops=64 * rows * rows * all_heads * head_dim,
            bytes_accessed=8 * state_pool.size,
            transcendentals=rows * rows * all_heads,
        ),
    )(
        order,
        *packed,
        *packed,
        select,
        moves,
        masks,
        history,
        history_state,
        taps,
        taps_state,
        skip_gain,
        steps,
        state_pool,
    )


def by_chunk(array, chunks, lanes):
    rows, width = array.shape
    parts = array.reshape(rows, chunks, width // chunks).transpose(1, 0, 2)
    return jnp.pad(parts, ((0, 0), (0, 0), (0, lanes - width // chunks)))


def swap(value, axis):
    return rotate(value, axis, 1)


def near_half(weight):
    me = lax.axis_index("near")
    keep = lax.dynamic_index_in_dim(weight, me, 0, keepdims=False)
    give = lax.dynamic_index_in_dim(weight, 1 - me, 0, keepdims=False)
    take = swap(give, "near")
    return jnp.concatenate([jnp.where(me == 0, keep, take), jnp.where(me == 0, take, keep)])


def tie(value, *others):
    return lax.optimization_barrier((value,) + others)[0]


def out_kernel(place_ref, own_ref, peer_ref, *refs):
    weight_refs, own_out_ref, both_out_ref = refs[:8], refs[8], refs[9]
    rows = own_ref.shape[0]
    both = jnp.concatenate([own_ref[...], peer_ref[...]], axis=0)
    for pair in range(4):
        weight = jnp.concatenate([weight_refs[2 * pair][...], weight_refs[2 * pair + 1][...]], axis=1)
        total = jnp.dot(both, weight, preferred_element_type=F32)
        for at in range(2):
            start = place_ref[(2 * pair + at) % 4] * LANES
            lanes = pl.ds(pl.multiple_of(start, LANES), LANES)
            columns = slice(at * LANES, (at + 1) * LANES)
            own_out_ref[pair // 2, :, lanes] = total[:rows, columns]
            for group in range(2):
                part = total[group * rows : (group + 1) * rows, columns]
                both_out_ref[pair // 2, group, :, lanes] = part.astype(BF16)


def project_out(own, peer, weights, place_of):
    rows, depth = own.shape
    whole = pl.BlockSpec(memory_space=pltpu.VMEM)
    return pl.pallas_call(
        out_kernel,
        in_specs=[pl.BlockSpec(memory_space=pltpu.SMEM)] + [whole] * 10,
        out_specs=[whole, whole],
        out_shape=[
            jax.ShapeDtypeStruct((2, rows, 4 * LANES), F32),
            jax.ShapeDtypeStruct((2, 2, rows, 4 * LANES), BF16),
        ],
        compiler_params=pltpu.CompilerParams(vmem_limit_bytes=24 * 1024 * 1024),
        cost_estimate=QUICK,
    )(place_of, own, peer, *weights)


def on_device(
    hidden_in,
    z_weight,
    x_weight,
    state_proj,
    step_weight,
    step_bias,
    decay_log,
    skip_gain,
    conv_inner,
    conv_state,
    norm_gain,
    out_weight,
    state_pool,
    conv_pool_inner,
    conv_pool_state,
    owner_dev,
    state_page,
    conv_page,
    accepted,
):
    groups = lax.axis_size(RING)
    fars, nears, sides, cores = (lax.axis_size(name) for name in RING)
    splits = lax.axis_size("mdl")
    paired = (fars, nears, sides, cores, splits) == (2, 2, 2, 2, 2)
    paired = paired and hidden_in.shape[1] == groups * LANES
    chunks = fars * nears if paired else nears
    this_dev = lax.axis_index(RING)
    near_at = lax.axis_index("near")
    me = lax.axis_index(SLABS) if paired else near_at
    part = lax.axis_index("mdl")
    per_dev, all_heads, head_dim, state_width = state_pool.shape
    rows, depth = hidden_in.shape
    draft = rows // per_dev
    inner = all_heads * head_dim
    slots = WINDOW * CAP
    chunk_width = inner // chunks
    lanes = chunk_width
    map_width = 2 * state_width // chunks
    heads = all_heads // chunks
    aux_lanes = round_up(map_width + heads, LANES)
    keep = KCONV - 1
    hist_rows = per_dev * keep
    hist_pad = round_up(hist_rows, 32)

    send_table, gather_table, conv_of, kept_count = route_tables(
        owner_dev, state_page, conv_page, accepted, groups, per_dev, this_dev
    )

    block = depth // groups
    columns = hidden_in.reshape(rows, fars, nears, sides, cores, block).transpose(0, 4, 3, 1, 2, 5)
    columns = columns.reshape(rows, splits, depth // splits)
    share = lax.dynamic_index_in_dim(columns, part, 1, keepdims=False)
    outgoing = one_hot_apply(send_table, share, (slots, draft, depth // splits))

    def prepare(after):
        conv_now, kept_now, pool_inner, pool_state, bias, rate = lax.optimization_barrier(
            (conv_of, kept_count, conv_pool_inner, conv_pool_state, step_bias, decay_log, after)
        )[:6]
        order = (jnp.arange(chunks, dtype=jnp.int32) - me) % chunks
        home_chunk = (jnp.arange(chunks, dtype=jnp.int32) + me) % chunks
        lane = jnp.arange(aux_lanes, dtype=jnp.int32)[None, :]
        step_lanes = round_up(all_heads, LANES)
        target = jnp.where(
            lane < map_width,
            home_chunk[:, None] * map_width + lane,
            jnp.where(
                lane < map_width + heads,
                2 * state_width + home_chunk[:, None] * heads + lane - map_width,
                -1,
            ),
        )
        select = (
            target[:, :, None] == jnp.arange(2 * state_width + step_lanes, dtype=jnp.int32)
        ).astype(BF16)
        tables = series_tables(conv_now, kept_now, per_dev, draft, hist_pad)
        pad_rows = ((0, hist_pad - hist_rows), (0, 0))
        history = jnp.pad(pool_inner.reshape(hist_rows, inner), pad_rows)
        history_state = jnp.pad(pool_state.reshape(hist_rows, 2 * state_width), pad_rows)
        pad_heads = ((0, 0), (0, step_lanes - all_heads))
        steps = jnp.pad(jnp.stack([bias, -jnp.exp(rate)]), pad_heads)
        return order, select, tables, history, history_state, steps

    def route(slots_out):
        return [
            rotate(slots_out[offset * CAP : (offset + 1) * CAP], RING, offset)
            for offset in range(WINDOW)
        ]

    packed_weight = jnp.concatenate(
        [
            by_chunk(x_weight, chunks, lanes),
            by_chunk(state_proj, chunks, map_width),
            by_chunk(step_weight, chunks, aux_lanes - map_width),
            by_chunk(z_weight, chunks, lanes),
        ],
        axis=2,
    )
    split = lanes + aux_lanes
    width = split + lanes
    far, side, core = (lax.axis_index(name) for name in ("far", "side", "core"))
    if paired:
        incoming = route(outgoing)
        packed_weight, early = lax.optimization_barrier((packed_weight, incoming[: WINDOW - 2]))
        pieces = [
            rotate(
                lax.dynamic_index_in_dim(packed_weight, (me + step) % chunks, 0, keepdims=False),
                SLABS,
                step,
            )
            for step in range(chunks)
        ]
        side_own = swap(pieces[0], "side")
        extras = prepare(early)
        incoming, pieces, side_own, extras = lax.optimization_barrier(
            (early + incoming[WINDOW - 2 :], pieces, side_own, extras)
        )
        owned = one_hot_apply(gather_table, jnp.concatenate(incoming), (rows, depth // splits))
        owned, pieces = lax.optimization_barrier((owned, pieces))
        rows_of = [rotate(owned, SLABS, step) for step in range(chunks)]
        slabs = [(me - step) % chunks for step in range(chunks)]
        across = swap(jnp.stack(pieces[1:]), "side")
        held = place(pieces, slabs)
        rows_of, across, held = lax.optimization_barrier((rows_of, across, held))
        out_far, out_side = swap(out_weight, "far"), swap(out_weight, "side")
        across = place([side_own] + [across[at] for at in range(chunks - 1)], slabs)
        held, across = held.reshape(-1, width), across.reshape(-1, width)
        weights = jnp.concatenate([held, across, swap(held, "core"), swap(across, "core")])
        early_own = jnp.concatenate(rows_of[1:3])
        late_own = jnp.concatenate([rows_of[3], rows_of[0]])
        early_peer = swap(early_own, "mdl")
        early_own, early_peer, late_own, weights, out_side = lax.optimization_barrier(
            (early_own, early_peer, late_own, weights, out_side)
        )

        def project(own, peer):
            low = jnp.where(part == core, own, peer)
            high = jnp.where(part == core, peer, own)
            quarter = depth // 4
            lhs = [
                lax.dynamic_slice_in_dim(value, at_side * quarter, quarter, 1)
                for value in (low, high)
                for at_side in (side, 1 - side)
            ]
            total = jnp.dot(jnp.concatenate(lhs, axis=1), weights, preferred_element_type=F32)
            return total.astype(BF16)

        late_peer = swap(late_own, "mdl")
        early = project(early_own, early_peer)
        packed_1 = rotate(early[:rows, :split], SLABS, -1)
        packed_2 = rotate(early[rows:, :split], SLABS, -2)
        late = project(late_own, late_peer)
        packed_3 = rotate(late[:rows, :split], SLABS, -3)
        early, late, packed_1, packed_2, packed_3, out_far = lax.optimization_barrier(
            (early, late, packed_1, packed_2, packed_3, out_far)
        )
        packed = [late[rows:, :split], packed_1, packed_2, packed_3]
        gate = [
            late[rows:, split:],
            rotate(early[:rows, split:], SLABS, -1),
            rotate(early[rows:, split:], SLABS, -2),
            rotate(late[:rows, split:], SLABS, -3),
        ]
        out_across = swap(out_far, "side")
        out_columns = []
        for column in (out_weight, out_side, out_far, out_across):
            out_columns += [column, swap(column, "core")]
    else:
        incoming = route(outgoing)
        extras = prepare(outgoing)
        owned = one_hot_apply(gather_table, jnp.concatenate(incoming), (rows, depth // splits))
        owned = lax.all_gather(owned, "mdl", axis=1, tiled=True)
        owned = jnp.concatenate([owned, swap(owned, "near")])
        weight = near_half(packed_weight)
        for name in ("far", "side", "core"):
            weight = lax.all_gather(weight, name, axis=0, tiled=True)
        total = jnp.dot(owned, weight, preferred_element_type=F32).astype(BF16)
        total = [total[:rows], swap(total[rows:], "near")]
        packed = [value[:, :split] for value in total]
        gate = [value[:, split:] for value in total]
        out_columns = lax.all_gather(out_weight, RING, axis=1, tiled=True)

    order, select, tables, history, history_state, steps = extras
    y_rows, picked, b_rows, ends, conv_rows, conv_state_rows = mix_requests(
        packed,
        order,
        select,
        tables,
        history,
        history_state,
        conv_inner,
        conv_state,
        skip_gain,
        steps,
        state_pool,
    )

    gate_here = []
    for chunk in range(chunks):
        value = gate[0]
        for step in range(1, chunks):
            value = jnp.where(me == (chunk - step) % chunks, gate[step], value)
        gate_here.append(value)
    gate_here = jnp.concatenate(gate_here, axis=1).astype(F32)
    gated = y_rows.astype(F32) * (gate_here / (1.0 + jnp.exp(-gate_here)))
    squares = jnp.sum(gated * gated, axis=1)
    scaled = (gated * norm_gain).astype(BF16)
    new_states = update_states(picked, tie(b_rows, scaled), ends, state_pool)
    wide = depth // splits
    total_inner = inner * splits
    if paired:
        squares = squares + swap(squares, "mdl")
        scale = lax.rsqrt(squares / total_inner + EPSILON)
        columns_at = jnp.stack(
            [2 * at_side + at_core for at_side in (side, 1 - side) for at_core in (core, 1 - core)]
        )
        terms, given = project_out(scaled, tie(swap(scaled, "near"), new_states), out_columns, columns_at)
        here = far == part
        mine = jnp.where(here, terms[0], terms[1])
        other = jnp.where(here, given[1, 0], given[0, 0])
        peer_mine = jnp.where(here, given[0, 1], given[1, 1])
        peer_other = jnp.where(here, given[1, 1], given[0, 1])
        over_y = swap(other, "mdl")
        over_near = swap(peer_mine, "near")
        over_both = lax.ppermute(peer_other, ("near", "mdl"), [(0, 3), (1, 2), (2, 1), (3, 0)])
        here = (mine + over_y.astype(F32)) * scale[:, None]
        there = (over_near.astype(F32) + over_both.astype(F32)) * scale[:, None]
        here, there = here.astype(BF16), there.astype(BF16)
        mixed_rows = jnp.concatenate(
            [jnp.where(near_at == 0, here, there), jnp.where(near_at == 0, there, here)], axis=1
        )
    else:
        terms = jnp.dot(scaled, out_columns, preferred_element_type=F32)
        squares = lax.psum(squares, "mdl")
        total = lax.psum_scatter(terms, "mdl", scatter_dimension=1, tiled=True)
        scale = lax.rsqrt(squares / total_inner + EPSILON)
        mixed_rows = (total * scale[:, None]).astype(BF16)

    returning = one_hot_apply(
        gather_table.T, mixed_rows.reshape(per_dev, draft, wide), (slots, draft, wide)
    )
    arrived = jnp.concatenate(
        [
            rotate(returning[offset * CAP : (offset + 1) * CAP], RING, -offset)
            for offset in range(WINDOW)
        ],
        axis=0,
    )
    mixed = one_hot_apply(send_table.T, arrived, (rows, wide))
    return (
        mixed,
        new_states,
        conv_rows[:hist_rows].reshape(per_dev, keep, inner),
        conv_state_rows[:hist_rows].reshape(per_dev, keep, 2 * state_width),
    )


def solution(mesh):
    sizes = factor(mesh.shape["req"])
    split_mesh = Mesh(mesh.devices.reshape(*sizes, mesh.shape["mdl"]), RING + ("mdl",))
    return jax.shard_map(
        on_device,
        mesh=split_mesh,
        in_specs=(
            P(RING, None),
            P(RING, "mdl"),
            P(RING, "mdl"),
            P(RING, None),
            P(RING, "mdl"),
            P("mdl"),
            P("mdl"),
            P("mdl"),
            P(None, "mdl"),
            P(),
            P("mdl"),
            P("mdl", RING),
            P(RING, "mdl", None, None),
            P(RING, None, "mdl"),
            P(RING, None, None),
            P(),
            P(),
            P(),
            P(),
        ),
        out_specs=(
            P(RING, "mdl"),
            P(RING, "mdl", None, None),
            P(RING, None, "mdl"),
            P(RING, None, None),
        ),
        check_vma=False,
    )
```

```python
import jax
import jax.numpy as jnp
from jax import lax
from jax.experimental import pallas as pl
from jax.experimental.pallas import tpu as pltpu
from jax.sharding import Mesh, PartitionSpec as P

KCONV = 4
CAP = 2
WINDOW = 8
LANES = 128
QUICK = pl.CostEstimate(flops=1000, bytes_accessed=1000, transcendentals=0)
VMEM_LIMIT = 56 * 1024 * 1024
EPSILON = 1e-05
HIGH = lax.Precision.HIGHEST
BF16 = jnp.bfloat16
F32 = jnp.float32

RING = ("far", "near", "side", "core")
SLABS = ("far", "near")


def round_up(value, unit):
    return -(-value // unit) * unit


def factor(count):
    core, near = 2, 2
    chips = count // core
    side = 1
    while (2 * side) ** 2 <= chips:
        side *= 2
    return chips // side // near, near, side, core


def rotate(value, axis, steps):
    count = lax.axis_size(axis)
    if steps % count == 0:
        return value
    pairs = [(source, (source + steps) % count) for source in range(count)]
    return lax.ppermute(value, axis, pairs)


def gather_axis(value, axis, dim):
    count = lax.axis_size(axis)
    if count == 1:
        return value
    if count > 2:
        return lax.all_gather(value, axis, axis=dim, tiled=True)
    peer = rotate(value, axis, 1)
    first = lax.axis_index(axis) == 0
    return jnp.concatenate(
        [jnp.where(first, value, peer), jnp.where(first, peer, value)], axis=dim
    )


def place(pieces, slots):
    full = jnp.zeros((len(pieces),) + pieces[0].shape, pieces[0].dtype)
    for piece, slot in zip(pieces, slots):
        full = lax.dynamic_update_slice_in_dim(full, piece[None], slot, 0)
    return full


def one_hot_apply(table, values, shape):
    flat = values.reshape(table.shape[1], -1)
    return jnp.dot(table, flat, preferred_element_type=F32).astype(BF16).reshape(shape)


def route_tables(owner_dev, state_page, conv_page, accepted, groups, per_dev, this_dev):
    owner_grid = owner_dev.reshape(groups, per_dev)
    home_grid = jnp.arange(groups, dtype=jnp.int32)[:, None]
    offset_grid = (owner_grid - home_grid + groups) % groups
    positions = jnp.arange(per_dev, dtype=jnp.int32)
    earlier = positions[None, :] < positions[:, None]
    pair_rank = jnp.sum((owner_grid[:, :, None] == owner_grid[:, None, :]) & earlier[None], axis=2)
    slot_grid = offset_grid * CAP + pair_rank
    send_at = lax.dynamic_slice_in_dim(slot_grid, this_dev, 1, 0)[0]
    buffer_rows = jnp.arange(WINDOW * CAP, dtype=jnp.int32)
    send_table = (buffer_rows[:, None] == send_at[None, :]).astype(BF16)
    arrive_at = slot_grid.reshape(-1)
    slot_match = (owner_dev[None, :] == this_dev) & (state_page[None, :] == positions[:, None])
    pick_from = jnp.sum(jnp.where(slot_match, arrive_at[None, :], 0), axis=1)
    conv_of = jnp.sum(jnp.where(slot_match, conv_page[None, :], 0), axis=1)
    kept_count = jnp.sum(jnp.where(slot_match, accepted[None, :], 0), axis=1)
    gather_table = (buffer_rows[None, :] == pick_from[:, None]).astype(BF16)
    return (send_table, gather_table, conv_of, kept_count)


def tables_kernel(sizes, conv_ref, kept_ref, moves_ref, masks_ref):
    per_dev, draft, hist_pad = sizes
    rows = per_dev * draft
    keep = KCONV - 1
    width = rows + hist_pad

    def pick(slot, scalars):
        return sum(jnp.where(slot == at, scalars[at], 0) for at in range(per_dev))

    row = lax.broadcasted_iota(jnp.int32, (rows, width), 0)
    column = lax.broadcasted_iota(jnp.int32, (rows, width), 1)
    step = row % draft
    page_row = pick(row // draft, conv_ref) * keep
    for delay in range(1, KCONV):
        source = jnp.where(step >= delay, row - delay, rows + page_row + keep + step - delay)
        moves_ref[(delay - 1) * rows : delay * rows, :] = (column == source).astype(F32).astype(BF16)
    out_row = lax.broadcasted_iota(jnp.int32, (hist_pad, width), 0)
    column = lax.broadcasted_iota(jnp.int32, (hist_pad, width), 1)
    out_page, out_at = out_row // keep, out_row % keep
    source = jnp.full((hist_pad, width), -1, jnp.int32)
    for slot in range(per_dev):
        at = kept_ref[slot] + out_at
        held = jnp.where(at < keep, rows + out_page * keep + at, slot * draft + at - keep)
        source = jnp.where(out_page == conv_ref[slot], held, source)
    moves_ref[keep * rows : keep * rows + hist_pad, :] = (column == source).astype(F32).astype(BF16)
    row = lax.broadcasted_iota(jnp.int32, (rows, rows), 0)
    column = lax.broadcasted_iota(jnp.int32, (rows, rows), 1)
    step = row % draft
    kept = pick(row // draft, kept_ref)
    masks_ref[0] = (step < kept).astype(F32)
    masks_ref[1] = (column == row - step + kept - 1).astype(F32)
    same = row // draft == column // draft
    masks_ref[2] = (same & (column <= row)).astype(F32)
    masks_ref[3] = (same & (column >= row)).astype(F32)


def series_tables(conv_of, kept_count, per_dev, draft, hist_pad):
    rows = per_dev * draft
    smem = pl.BlockSpec(memory_space=pltpu.SMEM)
    return pl.pallas_call(
        lambda *refs: tables_kernel((per_dev, draft, hist_pad), *refs),
        in_specs=[smem, smem],
        out_specs=[pl.BlockSpec(memory_space=pltpu.VMEM)] * 2,
        out_shape=[
            jax.ShapeDtypeStruct(((KCONV - 1) * rows + hist_pad, rows + hist_pad), BF16),
            jax.ShapeDtypeStruct((4, rows, rows), F32),
        ],
    )(conv_of, kept_count)


def split_pair(value):
    high = value.astype(BF16)
    return high, (value - high.astype(F32)).astype(BF16)


def convolve(series, current, taps, moves_ref):
    rows = current.shape[0]
    total = taps[KCONV - 1 : KCONV] * current
    for delay in range(1, KCONV):
        move = moves_ref[(delay - 1) * rows : delay * rows, :]
        moved = jnp.dot(move, series, preferred_element_type=F32)
        total = total + taps[KCONV - 1 - delay : KCONV - delay] * moved
    return total / (1.0 + jnp.exp(-total))


def mixer_kernel(sizes, order_ref, *refs):
    chunks, per_dev, draft, heads, head_dim, state_width = sizes
    x_refs, aux_refs, refs = refs[:chunks], refs[chunks : 2 * chunks], refs[2 * chunks :]
    (
        select_ref,
        moves_ref,
        masks_ref,
        hist_ref,
        hist_state_ref,
        taps_ref,
        taps_state_ref,
        skip_ref,
        step_ref,
        state_ref,
        y_ref,
        picked_ref,
        b_ref,
        end_ref,
        conv_ref,
        conv_state_ref,
        c_scr,
        scores_scr,
        log_scr,
        log_t_scr,
        step_t_scr,
        sel_t_scr,
    ) = refs
    rows = per_dev * draft
    width = heads * head_dim
    group = pl.program_id(0)
    edges = moves_ref[(KCONV - 1) * rows :, :]

    @pl.when(group == 0)
    def prepare():
        aux = jnp.dot(aux_refs[0][...], select_ref[0], preferred_element_type=F32)
        for chunk in range(1, chunks):
            aux = aux + jnp.dot(aux_refs[chunk][...], select_ref[chunk], preferred_element_type=F32)
        maps = aux[:, : 2 * state_width]
        series = jnp.concatenate([maps.astype(BF16), hist_state_ref[...]], axis=0)
        active = convolve(series, maps, taps_state_ref[...], moves_ref)
        conv_state_ref[...] = jnp.dot(edges, series, preferred_element_type=F32).astype(BF16)
        b_rows, c_rows = active[:, :state_width], active[:, state_width:]
        c_high, c_low = split_pair(c_rows.T)
        c_scr[:state_width, :rows] = c_high
        c_scr[:state_width, rows:] = c_low
        c_scr[state_width:, :rows] = c_high
        c_scr[state_width:, rows:] = jnp.zeros_like(c_low)
        b_ref[...] = b_rows
        scores_scr[...] = lax.dot_general(
            b_rows, c_rows, (((1,), (1,)), ((), ())), precision=HIGH, preferred_element_type=F32
        ) * masks_ref[3]
        raw = aux[:, 2 * state_width :] + step_ref[:1, :]
        step_size = jnp.maximum(raw, 0.0) + jnp.log1p(jnp.exp(-jnp.abs(raw)))
        log_decay = jnp.dot(
            masks_ref[2], step_size * step_ref[1:2, :], precision=HIGH, preferred_element_type=F32
        )
        end = jnp.dot(masks_ref[1], log_decay, precision=HIGH, preferred_element_type=F32)
        kept = masks_ref[0] > 0.0
        chosen = jnp.where(kept, jnp.exp(jnp.where(kept, end - log_decay, 0.0)), 0.0) * step_size
        end_ref[...] = jnp.exp(end)
        for chunk in range(chunks):
            log_scr[chunk] = log_decay[:, chunk * heads : (chunk + 1) * heads]
        log_t_scr[...] = log_decay.T
        step_t_scr[...] = step_size.T
        sel_t_scr[...] = chosen.T

    x_rows = x_refs[0][...]
    for chunk in range(1, chunks):
        x_rows = jnp.where(order_ref[group] == chunk, x_refs[chunk][...], x_rows)
    series = jnp.concatenate([x_rows, hist_ref[...]], axis=0)
    active = convolve(series, x_rows.astype(F32), taps_ref[...], moves_ref).T
    conv_ref[...] = jnp.dot(edges, series, preferred_element_type=F32).astype(BF16)
    log_here = log_scr[group]
    slot_of = lax.broadcasted_iota(jnp.int32, (width, rows), 1) // draft
    c_all = c_scr[...]
    carried = jnp.zeros((width, rows), F32)
    for slot in range(per_dev):
        high, low = split_pair(state_ref[slot].reshape(width, state_width))
        read = jnp.dot(jnp.concatenate([high, low], axis=1), c_all, preferred_element_type=F32)
        carried = jnp.where(slot_of == slot, read[:, :rows] + read[:, rows:], carried)
    outputs, picked = [], []
    for head in range(heads):
        part = slice(head * head_dim, (head + 1) * head_dim)
        at = group * heads + head
        log_row = log_t_scr[pl.ds(at, 1), :]
        spread = jnp.where(masks_ref[3] > 0.0, log_row - log_here[:, head : head + 1], -1e30)
        weight = (jnp.exp(spread) * scores_scr[...]).astype(BF16)
        x_head = active[part]
        within = jnp.dot(
            (x_head * step_t_scr[pl.ds(at, 1), :]).astype(BF16), weight, preferred_element_type=F32
        )
        outputs.append(within + jnp.exp(log_row) * carried[part] + skip_ref[at] * x_head)
        picked.append(x_head * sel_t_scr[pl.ds(at, 1), :])
    y_ref[...] = jnp.concatenate(outputs, axis=0).T.astype(BF16)
    x_high, x_low = split_pair(jnp.concatenate(picked, axis=0))
    picked_ref[:, :rows] = x_high
    picked_ref[:, rows:] = x_low


def update_kernel(sizes, picked_ref, b_ref, end_ref, state_ref, new_state_ref, b_scr, end_scr):
    steps, per_dev, draft, heads, head_dim, state_width = sizes
    rows = per_dev * draft
    group = pl.program_id(0)

    @pl.when(group == 0)
    def prepare():
        slot = lax.broadcasted_iota(jnp.int32, (rows, state_width), 0) // draft
        for at in range(per_dev):
            high, low = split_pair(jnp.where(slot == at, b_ref[...], 0.0))
            lanes = slice(at * state_width, (at + 1) * state_width)
            b_scr[:rows, lanes] = high
            b_scr[rows : 2 * rows, lanes] = high
            b_scr[2 * rows :, lanes] = low
        for step in range(steps):
            end_scr[step] = end_ref[:, step * heads : (step + 1) * heads]

    end_here = end_scr[group]
    picked = jnp.concatenate([picked_ref[...], picked_ref[:, :rows]], axis=1)
    for pair in range(0, per_dev, 2):
        update = jnp.dot(
            picked,
            b_scr[:, pair * state_width : (pair + 2) * state_width],
            preferred_element_type=F32,
        )
        for slot in range(pair, pair + 2):
            lanes = slice((slot - pair) * state_width, (slot - pair + 1) * state_width)
            for head in range(heads):
                part = slice(head * head_dim, (head + 1) * head_dim)
                keep = end_here[slot * draft : slot * draft + 1, head : head + 1]
                new_state_ref[slot, head] = keep * state_ref[slot, head] + update[part, lanes]


def update_states(picked, b_rows, ends, state_pool):
    per_dev, all_heads, head_dim, state_width = state_pool.shape
    rows = b_rows.shape[0]
    steps = 4
    heads = all_heads // steps
    sizes = (steps, per_dev, rows // per_dev, heads, head_dim, state_width)
    state_spec = pl.BlockSpec((per_dev, heads, head_dim, state_width), lambda group: (0, group, 0, 0))
    return pl.pallas_call(
        lambda *refs: update_kernel(sizes, *refs),
        grid=(steps,),
        in_specs=[
            pl.BlockSpec((heads * head_dim, 2 * rows), lambda group: (group, 0)),
            pl.BlockSpec(b_rows.shape, lambda group: (0, 0)),
            pl.BlockSpec(ends.shape, lambda group: (0, 0)),
            state_spec,
        ],
        out_specs=state_spec,
        scratch_shapes=[
            pltpu.VMEM((3 * rows, per_dev * state_width), BF16),
            pltpu.VMEM((steps, rows, heads), F32),
        ],
        out_shape=jax.ShapeDtypeStruct(state_pool.shape, F32),
        compiler_params=pltpu.CompilerParams(vmem_limit_bytes=VMEM_LIMIT),
        cost_estimate=pl.CostEstimate(
            flops=64 * rows * rows * all_heads * head_dim,
            bytes_accessed=8 * state_pool.size,
            transcendentals=0,
        ),
    )(picked, b_rows, ends, state_pool)


def mix_requests(
    packed,
    order,
    select,
    tables,
    history,
    history_state,
    taps,
    taps_state,
    skip_gain,
    steps,
    state_pool,
):
    rows, packed_width = packed[0].shape
    chunks = len(packed)
    per_dev, all_heads, head_dim, state_width = state_pool.shape
    hist_pad, inner = history.shape
    heads = all_heads // chunks
    draft = rows // per_dev
    lanes = inner // chunks
    aux_lanes = packed_width - lanes
    moves, masks = tables
    sizes = (chunks, per_dev, draft, heads, head_dim, state_width)

    def whole(array):
        zeros = (0,) * array.ndim
        return pl.BlockSpec(array.shape, lambda group, order_ref: zeros)

    def by_group(height):
        return pl.BlockSpec((height, lanes), lambda group, order_ref: (0, group))

    x_spec = pl.BlockSpec((rows, lanes), lambda group, order_ref: (0, 0))
    aux_spec = pl.BlockSpec(
        (rows, aux_lanes), lambda group, order_ref: (0, lanes // aux_lanes)
    )

    state_spec = pl.BlockSpec(
        (per_dev, heads, head_dim, state_width), lambda group, order_ref: (0, group, 0, 0)
    )
    step_lanes = select.shape[2] - 2 * state_width
    grid_spec = pltpu.PrefetchScalarGridSpec(
        num_scalar_prefetch=1,
        grid=(chunks,),
        in_specs=[
            *[x_spec] * chunks,
            *[aux_spec] * chunks,
            whole(select),
            whole(moves),
            whole(masks),
            by_group(hist_pad),
            whole(history_state),
            by_group(KCONV),
            whole(taps_state),
            pl.BlockSpec(memory_space=pltpu.SMEM),
            whole(steps),
            state_spec,
        ],
        out_specs=[
            by_group(rows),
            pl.BlockSpec((heads * head_dim, 2 * rows), lambda group, order_ref: (group, 0)),
            pl.BlockSpec((rows, state_width), lambda group, order_ref: (0, 0)),
            pl.BlockSpec((rows, step_lanes), lambda group, order_ref: (0, 0)),
            by_group(hist_pad),
            pl.BlockSpec((hist_pad, 2 * state_width), lambda group, order_ref: (0, 0)),
        ],
        scratch_shapes=[
            pltpu.VMEM((2 * state_width, 2 * rows), BF16),
            pltpu.VMEM((rows, rows), F32),
            pltpu.VMEM((chunks, rows, heads), F32),
            pltpu.VMEM((step_lanes, rows), F32),
            pltpu.VMEM((step_lanes, rows), F32),
            pltpu.VMEM((step_lanes, rows), F32),
        ],
    )
    return pl.pallas_call(
        lambda *refs: mixer_kernel(sizes, *refs),
        grid_spec=grid_spec,
        out_shape=(
            jax.ShapeDtypeStruct((rows, inner), BF16),
            jax.ShapeDtypeStruct((inner, 2 * rows), BF16),
            jax.ShapeDtypeStruct((rows, state_width), F32),
            jax.ShapeDtypeStruct((rows, step_lanes), F32),
            jax.ShapeDtypeStruct((hist_pad, inner), BF16),
            jax.ShapeDtypeStruct((hist_pad, 2 * state_width), BF16),
        ),
        compiler_params=pltpu.CompilerParams(vmem_limit_bytes=VMEM_LIMIT),
        cost_estimate=pl.CostEstimate(
            flops=64 * rows * rows * all_heads * head_dim,
            bytes_accessed=8 * state_pool.size,
            transcendentals=rows * rows * all_heads,
        ),
    )(
        order,
        *packed,
        *packed,
        select,
        moves,
        masks,
        history,
        history_state,
        taps,
        taps_state,
        skip_gain,
        steps,
        state_pool,
    )


def by_chunk(array, chunks, lanes):
    rows, width = array.shape
    parts = array.reshape(rows, chunks, width // chunks).transpose(1, 0, 2)
    return jnp.pad(parts, ((0, 0), (0, 0), (0, lanes - width // chunks)))


def swap(value, axis):
    return rotate(value, axis, 1)


def near_half(weight):
    me = lax.axis_index("near")
    keep = lax.dynamic_index_in_dim(weight, me, 0, keepdims=False)
    give = lax.dynamic_index_in_dim(weight, 1 - me, 0, keepdims=False)
    take = swap(give, "near")
    return jnp.concatenate([jnp.where(me == 0, keep, take), jnp.where(me == 0, take, keep)])


def tie(value, *others):
    return lax.optimization_barrier((value,) + others)[0]


def out_kernel(place_ref, own_ref, peer_ref, *refs):
    weight_refs, own_out_ref, both_out_ref = refs[:8], refs[8], refs[9]
    rows = own_ref.shape[0]
    both = jnp.concatenate([own_ref[...], peer_ref[...]], axis=0)
    for pair in range(4):
        weight = jnp.concatenate([weight_refs[2 * pair][...], weight_refs[2 * pair + 1][...]], axis=1)
        total = jnp.dot(both, weight, preferred_element_type=F32)
        for at in range(2):
            start = place_ref[(2 * pair + at) % 4] * LANES
            lanes = pl.ds(pl.multiple_of(start, LANES), LANES)
            columns = slice(at * LANES, (at + 1) * LANES)
            own_out_ref[pair // 2, :, lanes] = total[:rows, columns]
            for group in range(2):
                part = total[group * rows : (group + 1) * rows, columns]
                both_out_ref[pair // 2, group, :, lanes] = part.astype(BF16)


def project_out(own, peer, weights, place_of):
    rows, depth = own.shape
    whole = pl.BlockSpec(memory_space=pltpu.VMEM)
    return pl.pallas_call(
        out_kernel,
        in_specs=[pl.BlockSpec(memory_space=pltpu.SMEM)] + [whole] * 10,
        out_specs=[whole, whole],
        out_shape=[
            jax.ShapeDtypeStruct((2, rows, 4 * LANES), F32),
            jax.ShapeDtypeStruct((2, 2, rows, 4 * LANES), BF16),
        ],
        compiler_params=pltpu.CompilerParams(vmem_limit_bytes=24 * 1024 * 1024),
        cost_estimate=QUICK,
    )(place_of, own, peer, *weights)


def on_device(
    hidden_in,
    z_weight,
    x_weight,
    state_proj,
    step_weight,
    step_bias,
    decay_log,
    skip_gain,
    conv_inner,
    conv_state,
    norm_gain,
    out_weight,
    state_pool,
    conv_pool_inner,
    conv_pool_state,
    owner_dev,
    state_page,
    conv_page,
    accepted,
):
    groups = lax.axis_size(RING)
    fars, nears, sides, cores = (lax.axis_size(name) for name in RING)
    splits = lax.axis_size("mdl")
    paired = (fars, nears, sides, cores, splits) == (2, 2, 2, 2, 2)
    paired = paired and hidden_in.shape[1] == groups * LANES
    chunks = fars * nears if paired else nears
    this_dev = lax.axis_index(RING)
    near_at = lax.axis_index("near")
    me = lax.axis_index(SLABS) if paired else near_at
    part = lax.axis_index("mdl")
    per_dev, all_heads, head_dim, state_width = state_pool.shape
    rows, depth = hidden_in.shape
    draft = rows // per_dev
    inner = all_heads * head_dim
    slots = WINDOW * CAP
    chunk_width = inner // chunks
    lanes = chunk_width
    map_width = 2 * state_width // chunks
    heads = all_heads // chunks
    aux_lanes = round_up(map_width + heads, LANES)
    keep = KCONV - 1
    hist_rows = per_dev * keep
    hist_pad = round_up(hist_rows, 32)

    send_table, gather_table, conv_of, kept_count = route_tables(
        owner_dev, state_page, conv_page, accepted, groups, per_dev, this_dev
    )

    block = depth // groups
    columns = hidden_in.reshape(rows, fars, nears, sides, cores, block).transpose(0, 4, 3, 1, 2, 5)
    columns = columns.reshape(rows, splits, depth // splits)
    share = lax.dynamic_index_in_dim(columns, part, 1, keepdims=False)
    outgoing = one_hot_apply(send_table, share, (slots, draft, depth // splits))

    def prepare(after):
        conv_now, kept_now, pool_inner, pool_state, bias, rate = lax.optimization_barrier(
            (conv_of, kept_count, conv_pool_inner, conv_pool_state, step_bias, decay_log, after)
        )[:6]
        order = (jnp.arange(chunks, dtype=jnp.int32) - me) % chunks
        home_chunk = (jnp.arange(chunks, dtype=jnp.int32) + me) % chunks
        lane = jnp.arange(aux_lanes, dtype=jnp.int32)[None, :]
        step_lanes = round_up(all_heads, LANES)
        target = jnp.where(
            lane < map_width,
            home_chunk[:, None] * map_width + lane,
            jnp.where(
                lane < map_width + heads,
                2 * state_width + home_chunk[:, None] * heads + lane - map_width,
                -1,
            ),
        )
        select = (
            target[:, :, None] == jnp.arange(2 * state_width + step_lanes, dtype=jnp.int32)
        ).astype(BF16)
        tables = series_tables(conv_now, kept_now, per_dev, draft, hist_pad)
        pad_rows = ((0, hist_pad - hist_rows), (0, 0))
        history = jnp.pad(pool_inner.reshape(hist_rows, inner), pad_rows)
        history_state = jnp.pad(pool_state.reshape(hist_rows, 2 * state_width), pad_rows)
        pad_heads = ((0, 0), (0, step_lanes - all_heads))
        steps = jnp.pad(jnp.stack([bias, -jnp.exp(rate)]), pad_heads)
        return order, select, tables, history, history_state, steps

    def route(slots_out):
        return [
            rotate(slots_out[offset * CAP : (offset + 1) * CAP], RING, offset)
            for offset in range(WINDOW)
        ]

    packed_weight = jnp.concatenate(
        [
            by_chunk(x_weight, chunks, lanes),
            by_chunk(state_proj, chunks, map_width),
            by_chunk(step_weight, chunks, aux_lanes - map_width),
            by_chunk(z_weight, chunks, lanes),
        ],
        axis=2,
    )
    split = lanes + aux_lanes
    width = split + lanes
    far, side, core = (lax.axis_index(name) for name in ("far", "side", "core"))
    if paired:
        incoming = route(outgoing)
        packed_weight, early = lax.optimization_barrier((packed_weight, incoming[: WINDOW - 2]))
        pieces = [
            rotate(
                lax.dynamic_index_in_dim(packed_weight, (me + step) % chunks, 0, keepdims=False),
                SLABS,
                step,
            )
            for step in range(chunks)
        ]
        side_own = swap(pieces[0], "side")
        extras = prepare(early)
        incoming, pieces, side_own, extras = lax.optimization_barrier(
            (early + incoming[WINDOW - 2 :], pieces, side_own, extras)
        )
        owned = one_hot_apply(gather_table, jnp.concatenate(incoming), (rows, depth // splits))
        owned, pieces = lax.optimization_barrier((owned, pieces))
        rows_of = [rotate(owned, SLABS, step) for step in range(chunks)]
        slabs = [(me - step) % chunks for step in range(chunks)]
        across = swap(jnp.stack(pieces[1:]), "side")
        held = place(pieces, slabs)
        rows_of, across, held = lax.optimization_barrier((rows_of, across, held))
        out_far, out_side = swap(out_weight, "far"), swap(out_weight, "side")
        across = place([side_own] + [across[at] for at in range(chunks - 1)], slabs)
        held, across = held.reshape(-1, width), across.reshape(-1, width)
        weights = jnp.concatenate([held, across, swap(held, "core"), swap(across, "core")])
        early_own = jnp.concatenate(rows_of[1:3])
        late_own = jnp.concatenate([rows_of[3], rows_of[0]])
        early_peer = swap(early_own, "mdl")
        early_own, early_peer, late_own, weights, out_side = lax.optimization_barrier(
            (early_own, early_peer, late_own, weights, out_side)
        )

        def project(own, peer):
            low = jnp.where(part == core, own, peer)
            high = jnp.where(part == core, peer, own)
            quarter = depth // 4
            lhs = [
                lax.dynamic_slice_in_dim(value, at_side * quarter, quarter, 1)
                for value in (low, high)
                for at_side in (side, 1 - side)
            ]
            total = jnp.dot(jnp.concatenate(lhs, axis=1), weights, preferred_element_type=F32)
            return total.astype(BF16)

        late_peer = swap(late_own, "mdl")
        early = project(early_own, early_peer)
        packed_1 = rotate(early[:rows, :split], SLABS, -1)
        packed_2 = rotate(early[rows:, :split], SLABS, -2)
        late = project(late_own, late_peer)
        packed_3 = rotate(late[:rows, :split], SLABS, -3)
        out_across = swap(tie(out_far, late), "side")
        gate = [late[rows:, split:], early[:rows, split:], early[rows:, split:], late[:rows, split:]]
        packed = [late[rows:, :split], packed_1, packed_2, packed_3]
        gate, packed = lax.optimization_barrier((gate, packed))
        gate = [rotate(value, SLABS, -step) for step, value in enumerate(gate)]
        out_columns = []
        for column in (out_weight, out_side, out_far, out_across):
            out_columns += [column, swap(column, "core")]
    else:
        incoming = route(outgoing)
        extras = prepare(outgoing)
        owned = one_hot_apply(gather_table, jnp.concatenate(incoming), (rows, depth // splits))
        owned = lax.all_gather(owned, "mdl", axis=1, tiled=True)
        owned = jnp.concatenate([owned, swap(owned, "near")])
        weight = near_half(packed_weight)
        for name in ("far", "side", "core"):
            weight = lax.all_gather(weight, name, axis=0, tiled=True)
        total = jnp.dot(owned, weight, preferred_element_type=F32).astype(BF16)
        total = [total[:rows], swap(total[rows:], "near")]
        packed = [value[:, :split] for value in total]
        gate = [value[:, split:] for value in total]
        out_columns = lax.all_gather(out_weight, RING, axis=1, tiled=True)

    order, select, tables, history, history_state, steps = extras
    y_rows, picked, b_rows, ends, conv_rows, conv_state_rows = mix_requests(
        packed,
        order,
        select,
        tables,
        history,
        history_state,
        conv_inner,
        conv_state,
        skip_gain,
        steps,
        state_pool,
    )

    gate_here = []
    for chunk in range(chunks):
        value = gate[0]
        for step in range(1, chunks):
            value = jnp.where(me == (chunk - step) % chunks, gate[step], value)
        gate_here.append(value)
    gate_here = jnp.concatenate(gate_here, axis=1).astype(F32)
    gated = y_rows.astype(F32) * (gate_here / (1.0 + jnp.exp(-gate_here)))
    squares = jnp.sum(gated * gated, axis=1)
    scaled = (gated * norm_gain).astype(BF16)
    new_states = update_states(picked, tie(b_rows, scaled), ends, state_pool)
    wide = depth // splits
    total_inner = inner * splits
    if paired:
        squares = squares + swap(squares, "mdl")
        scale = lax.rsqrt(squares / total_inner + EPSILON)
        columns_at = jnp.stack(
            [2 * at_side + at_core for at_side in (side, 1 - side) for at_core in (core, 1 - core)]
        )
        terms, given = project_out(scaled, tie(swap(scaled, "near"), new_states), out_columns, columns_at)
        here = far == part
        mine = jnp.where(here, terms[0], terms[1])
        other = jnp.where(here, given[1, 0], given[0, 0])
        peer_mine = jnp.where(here, given[0, 1], given[1, 1])
        peer_other = jnp.where(here, given[1, 1], given[0, 1])
        over_y = swap(other, "mdl")
        over_near = swap(peer_mine, "near")
        over_both = lax.ppermute(peer_other, ("near", "mdl"), [(0, 3), (1, 2), (2, 1), (3, 0)])
        here = (mine + over_y.astype(F32)) * scale[:, None]
        there = (over_near.astype(F32) + over_both.astype(F32)) * scale[:, None]
        here, there = here.astype(BF16), there.astype(BF16)
        mixed_rows = jnp.concatenate(
            [jnp.where(near_at == 0, here, there), jnp.where(near_at == 0, there, here)], axis=1
        )
    else:
        terms = jnp.dot(scaled, out_columns, preferred_element_type=F32)
        squares = lax.psum(squares, "mdl")
        total = lax.psum_scatter(terms, "mdl", scatter_dimension=1, tiled=True)
        scale = lax.rsqrt(squares / total_inner + EPSILON)
        mixed_rows = (total * scale[:, None]).astype(BF16)

    returning = one_hot_apply(
        gather_table.T, mixed_rows.reshape(per_dev, draft, wide), (slots, draft, wide)
    )
    arrived = jnp.concatenate(
        [
            rotate(returning[offset * CAP : (offset + 1) * CAP], RING, -offset)
            for offset in range(WINDOW)
        ],
        axis=0,
    )
    mixed = one_hot_apply(send_table.T, arrived, (rows, wide))
    return (
        mixed,
        new_states,
        conv_rows[:hist_rows].reshape(per_dev, keep, inner),
        conv_state_rows[:hist_rows].reshape(per_dev, keep, 2 * state_width),
    )


def solution(mesh):
    sizes = factor(mesh.shape["req"])
    split_mesh = Mesh(mesh.devices.reshape(*sizes, mesh.shape["mdl"]), RING + ("mdl",))
    return jax.shard_map(
        on_device,
        mesh=split_mesh,
        in_specs=(
            P(RING, None),
            P(RING, "mdl"),
            P(RING, "mdl"),
            P(RING, None),
            P(RING, "mdl"),
            P("mdl"),
            P("mdl"),
            P("mdl"),
            P(None, "mdl"),
            P(),
            P("mdl"),
            P("mdl", RING),
            P(RING, "mdl", None, None),
            P(RING, None, "mdl"),
            P(RING, None, None),
            P(),
            P(),
            P(),
            P(),
        ),
        out_specs=(
            P(RING, "mdl"),
            P(RING, "mdl", None, None),
            P(RING, None, "mdl"),
            P(RING, None, None),
        ),
        check_vma=False,
    )
```

```python
import jax
import jax.numpy as jnp
from jax import lax
from jax.experimental import pallas as pl
from jax.experimental.pallas import tpu as pltpu
from jax.sharding import Mesh, PartitionSpec as P

KCONV = 4
CAP = 2
WINDOW = 8
LANES = 128
QUICK = pl.CostEstimate(flops=1000, bytes_accessed=1000, transcendentals=0)
VMEM_LIMIT = 56 * 1024 * 1024
EPSILON = 1e-05
HIGH = lax.Precision.HIGHEST
BF16 = jnp.bfloat16
F32 = jnp.float32

RING = ("far", "near", "side", "core")
SLABS = ("far", "near")


def round_up(value, unit):
    return -(-value // unit) * unit


def factor(count):
    core, near = 2, 2
    chips = count // core
    side = 1
    while (2 * side) ** 2 <= chips:
        side *= 2
    return chips // side // near, near, side, core


def rotate(value, axis, steps):
    count = lax.axis_size(axis)
    if steps % count == 0:
        return value
    pairs = [(source, (source + steps) % count) for source in range(count)]
    return lax.ppermute(value, axis, pairs)


def gather_axis(value, axis, dim):
    count = lax.axis_size(axis)
    if count == 1:
        return value
    if count > 2:
        return lax.all_gather(value, axis, axis=dim, tiled=True)
    peer = rotate(value, axis, 1)
    first = lax.axis_index(axis) == 0
    return jnp.concatenate(
        [jnp.where(first, value, peer), jnp.where(first, peer, value)], axis=dim
    )


def place(pieces, slots):
    full = jnp.zeros((len(pieces),) + pieces[0].shape, pieces[0].dtype)
    for piece, slot in zip(pieces, slots):
        full = lax.dynamic_update_slice_in_dim(full, piece[None], slot, 0)
    return full


def one_hot_apply(table, values, shape):
    flat = values.reshape(table.shape[1], -1)
    return jnp.dot(table, flat, preferred_element_type=F32).astype(BF16).reshape(shape)


def route_tables(owner_dev, state_page, conv_page, accepted, groups, per_dev, this_dev):
    owner_grid = owner_dev.reshape(groups, per_dev)
    home_grid = jnp.arange(groups, dtype=jnp.int32)[:, None]
    offset_grid = (owner_grid - home_grid + groups) % groups
    positions = jnp.arange(per_dev, dtype=jnp.int32)
    earlier = positions[None, :] < positions[:, None]
    pair_rank = jnp.sum((owner_grid[:, :, None] == owner_grid[:, None, :]) & earlier[None], axis=2)
    slot_grid = offset_grid * CAP + pair_rank
    send_at = lax.dynamic_slice_in_dim(slot_grid, this_dev, 1, 0)[0]
    buffer_rows = jnp.arange(WINDOW * CAP, dtype=jnp.int32)
    send_table = (buffer_rows[:, None] == send_at[None, :]).astype(BF16)
    arrive_at = slot_grid.reshape(-1)
    slot_match = (owner_dev[None, :] == this_dev) & (state_page[None, :] == positions[:, None])
    pick_from = jnp.sum(jnp.where(slot_match, arrive_at[None, :], 0), axis=1)
    conv_of = jnp.sum(jnp.where(slot_match, conv_page[None, :], 0), axis=1)
    kept_count = jnp.sum(jnp.where(slot_match, accepted[None, :], 0), axis=1)
    gather_table = (buffer_rows[None, :] == pick_from[:, None]).astype(BF16)
    return (send_table, gather_table, conv_of, kept_count)


def tables_kernel(sizes, conv_ref, kept_ref, moves_ref, masks_ref):
    per_dev, draft, hist_pad = sizes
    rows = per_dev * draft
    keep = KCONV - 1
    width = rows + hist_pad

    def pick(slot, scalars):
        return sum(jnp.where(slot == at, scalars[at], 0) for at in range(per_dev))

    row = lax.broadcasted_iota(jnp.int32, (rows, width), 0)
    column = lax.broadcasted_iota(jnp.int32, (rows, width), 1)
    step = row % draft
    page_row = pick(row // draft, conv_ref) * keep
    for delay in range(1, KCONV):
        source = jnp.where(step >= delay, row - delay, rows + page_row + keep + step - delay)
        moves_ref[(delay - 1) * rows : delay * rows, :] = (column == source).astype(F32).astype(BF16)
    out_row = lax.broadcasted_iota(jnp.int32, (hist_pad, width), 0)
    column = lax.broadcasted_iota(jnp.int32, (hist_pad, width), 1)
    out_page, out_at = out_row // keep, out_row % keep
    source = jnp.full((hist_pad, width), -1, jnp.int32)
    for slot in range(per_dev):
        at = kept_ref[slot] + out_at
        held = jnp.where(at < keep, rows + out_page * keep + at, slot * draft + at - keep)
        source = jnp.where(out_page == conv_ref[slot], held, source)
    moves_ref[keep * rows : keep * rows + hist_pad, :] = (column == source).astype(F32).astype(BF16)
    row = lax.broadcasted_iota(jnp.int32, (rows, rows), 0)
    column = lax.broadcasted_iota(jnp.int32, (rows, rows), 1)
    step = row % draft
    kept = pick(row // draft, kept_ref)
    masks_ref[0] = (step < kept).astype(F32)
    masks_ref[1] = (column == row - step + kept - 1).astype(F32)
    same = row // draft == column // draft
    masks_ref[2] = (same & (column <= row)).astype(F32)
    masks_ref[3] = (same & (column >= row)).astype(F32)


def series_tables(conv_of, kept_count, per_dev, draft, hist_pad):
    rows = per_dev * draft
    smem = pl.BlockSpec(memory_space=pltpu.SMEM)
    return pl.pallas_call(
        lambda *refs: tables_kernel((per_dev, draft, hist_pad), *refs),
        in_specs=[smem, smem],
        out_specs=[pl.BlockSpec(memory_space=pltpu.VMEM)] * 2,
        out_shape=[
            jax.ShapeDtypeStruct(((KCONV - 1) * rows + hist_pad, rows + hist_pad), BF16),
            jax.ShapeDtypeStruct((4, rows, rows), F32),
        ],
    )(conv_of, kept_count)


def split_pair(value):
    high = value.astype(BF16)
    return high, (value - high.astype(F32)).astype(BF16)


def convolve(series, current, taps, moves_ref):
    rows = current.shape[0]
    total = taps[KCONV - 1 : KCONV] * current
    for delay in range(1, KCONV):
        move = moves_ref[(delay - 1) * rows : delay * rows, :]
        moved = jnp.dot(move, series, preferred_element_type=F32)
        total = total + taps[KCONV - 1 - delay : KCONV - delay] * moved
    return total / (1.0 + jnp.exp(-total))


def mixer_kernel(sizes, order_ref, *refs):
    chunks, per_dev, draft, heads, head_dim, state_width = sizes
    x_refs, aux_refs, refs = refs[:chunks], refs[chunks : 2 * chunks], refs[2 * chunks :]
    (
        select_ref,
        moves_ref,
        masks_ref,
        hist_ref,
        hist_state_ref,
        taps_ref,
        taps_state_ref,
        skip_ref,
        step_ref,
        state_ref,
        y_ref,
        picked_ref,
        b_ref,
        end_ref,
        conv_ref,
        conv_state_ref,
        c_scr,
        scores_scr,
        log_scr,
        log_t_scr,
        step_t_scr,
        sel_t_scr,
    ) = refs
    rows = per_dev * draft
    width = heads * head_dim
    group = pl.program_id(0)
    edges = moves_ref[(KCONV - 1) * rows :, :]

    @pl.when(group == 0)
    def prepare():
        aux = jnp.dot(aux_refs[0][...], select_ref[0], preferred_element_type=F32)
        for chunk in range(1, chunks):
            aux = aux + jnp.dot(aux_refs[chunk][...], select_ref[chunk], preferred_element_type=F32)
        maps = aux[:, : 2 * state_width]
        series = jnp.concatenate([maps.astype(BF16), hist_state_ref[...]], axis=0)
        active = convolve(series, maps, taps_state_ref[...], moves_ref)
        conv_state_ref[...] = jnp.dot(edges, series, preferred_element_type=F32).astype(BF16)
        b_rows, c_rows = active[:, :state_width], active[:, state_width:]
        c_high, c_low = split_pair(c_rows.T)
        c_scr[:state_width, :rows] = c_high
        c_scr[:state_width, rows:] = c_low
        c_scr[state_width:, :rows] = c_high
        c_scr[state_width:, rows:] = jnp.zeros_like(c_low)
        b_ref[...] = b_rows
        scores_scr[...] = lax.dot_general(
            b_rows, c_rows, (((1,), (1,)), ((), ())), precision=HIGH, preferred_element_type=F32
        ) * masks_ref[3]
        raw = aux[:, 2 * state_width :] + step_ref[:1, :]
        step_size = jnp.maximum(raw, 0.0) + jnp.log1p(jnp.exp(-jnp.abs(raw)))
        log_decay = jnp.dot(
            masks_ref[2], step_size * step_ref[1:2, :], precision=HIGH, preferred_element_type=F32
        )
        end = jnp.dot(masks_ref[1], log_decay, precision=HIGH, preferred_element_type=F32)
        kept = masks_ref[0] > 0.0
        chosen = jnp.where(kept, jnp.exp(jnp.where(kept, end - log_decay, 0.0)), 0.0) * step_size
        end_ref[...] = jnp.exp(end)
        for chunk in range(chunks):
            log_scr[chunk] = log_decay[:, chunk * heads : (chunk + 1) * heads]
        log_t_scr[...] = log_decay.T
        step_t_scr[...] = step_size.T
        sel_t_scr[...] = chosen.T

    x_rows = x_refs[0][...]
    for chunk in range(1, chunks):
        x_rows = jnp.where(order_ref[group] == chunk, x_refs[chunk][...], x_rows)
    series = jnp.concatenate([x_rows, hist_ref[...]], axis=0)
    active = convolve(series, x_rows.astype(F32), taps_ref[...], moves_ref).T
    conv_ref[...] = jnp.dot(edges, series, preferred_element_type=F32).astype(BF16)
    log_here = log_scr[group]
    slot_of = lax.broadcasted_iota(jnp.int32, (width, rows), 1) // draft
    c_all = c_scr[...]
    carried = jnp.zeros((width, rows), F32)
    for slot in range(per_dev):
        high, low = split_pair(state_ref[slot].reshape(width, state_width))
        read = jnp.dot(jnp.concatenate([high, low], axis=1), c_all, preferred_element_type=F32)
        carried = jnp.where(slot_of == slot, read[:, :rows] + read[:, rows:], carried)
    outputs, picked = [], []
    for head in range(heads):
        part = slice(head * head_dim, (head + 1) * head_dim)
        at = group * heads + head
        log_row = log_t_scr[pl.ds(at, 1), :]
        spread = jnp.where(masks_ref[3] > 0.0, log_row - log_here[:, head : head + 1], -1e30)
        weight = (jnp.exp(spread) * scores_scr[...]).astype(BF16)
        x_head = active[part]
        within = jnp.dot(
            (x_head * step_t_scr[pl.ds(at, 1), :]).astype(BF16), weight, preferred_element_type=F32
        )
        outputs.append(within + jnp.exp(log_row) * carried[part] + skip_ref[at] * x_head)
        picked.append(x_head * sel_t_scr[pl.ds(at, 1), :])
    y_ref[...] = jnp.concatenate(outputs, axis=0).T.astype(BF16)
    x_high, x_low = split_pair(jnp.concatenate(picked, axis=0))
    picked_ref[:, :rows] = x_high
    picked_ref[:, rows:] = x_low


def update_kernel(sizes, picked_ref, b_ref, end_ref, state_ref, new_state_ref, b_scr, end_scr):
    steps, per_dev, draft, heads, head_dim, state_width = sizes
    rows = per_dev * draft
    group = pl.program_id(0)

    @pl.when(group == 0)
    def prepare():
        slot = lax.broadcasted_iota(jnp.int32, (rows, state_width), 0) // draft
        for at in range(per_dev):
            high, low = split_pair(jnp.where(slot == at, b_ref[...], 0.0))
            lanes = slice(at * state_width, (at + 1) * state_width)
            b_scr[:rows, lanes] = high
            b_scr[rows : 2 * rows, lanes] = high
            b_scr[2 * rows :, lanes] = low
        for step in range(steps):
            end_scr[step] = end_ref[:, step * heads : (step + 1) * heads]

    end_here = end_scr[group]
    picked = jnp.concatenate([picked_ref[...], picked_ref[:, :rows]], axis=1)
    for pair in range(0, per_dev, 2):
        update = jnp.dot(
            picked,
            b_scr[:, pair * state_width : (pair + 2) * state_width],
            preferred_element_type=F32,
        )
        for slot in range(pair, pair + 2):
            lanes = slice((slot - pair) * state_width, (slot - pair + 1) * state_width)
            for head in range(heads):
                part = slice(head * head_dim, (head + 1) * head_dim)
                keep = end_here[slot * draft : slot * draft + 1, head : head + 1]
                new_state_ref[slot, head] = keep * state_ref[slot, head] + update[part, lanes]


def update_states(picked, b_rows, ends, state_pool):
    per_dev, all_heads, head_dim, state_width = state_pool.shape
    rows = b_rows.shape[0]
    steps = 4
    heads = all_heads // steps
    sizes = (steps, per_dev, rows // per_dev, heads, head_dim, state_width)
    state_spec = pl.BlockSpec((per_dev, heads, head_dim, state_width), lambda group: (0, group, 0, 0))
    return pl.pallas_call(
        lambda *refs: update_kernel(sizes, *refs),
        grid=(steps,),
        in_specs=[
            pl.BlockSpec((heads * head_dim, 2 * rows), lambda group: (group, 0)),
            pl.BlockSpec(b_rows.shape, lambda group: (0, 0)),
            pl.BlockSpec(ends.shape, lambda group: (0, 0)),
            state_spec,
        ],
        out_specs=state_spec,
        scratch_shapes=[
            pltpu.VMEM((3 * rows, per_dev * state_width), BF16),
            pltpu.VMEM((steps, rows, heads), F32),
        ],
        out_shape=jax.ShapeDtypeStruct(state_pool.shape, F32),
        compiler_params=pltpu.CompilerParams(vmem_limit_bytes=VMEM_LIMIT),
        cost_estimate=pl.CostEstimate(
            flops=64 * rows * rows * all_heads * head_dim,
            bytes_accessed=8 * state_pool.size,
            transcendentals=0,
        ),
    )(picked, b_rows, ends, state_pool)


def mix_requests(
    packed,
    order,
    select,
    tables,
    history,
    history_state,
    taps,
    taps_state,
    skip_gain,
    steps,
    state_pool,
):
    rows, packed_width = packed[0].shape
    chunks = len(packed)
    per_dev, all_heads, head_dim, state_width = state_pool.shape
    hist_pad, inner = history.shape
    heads = all_heads // chunks
    draft = rows // per_dev
    lanes = inner // chunks
    aux_lanes = packed_width - lanes
    moves, masks = tables
    sizes = (chunks, per_dev, draft, heads, head_dim, state_width)

    def whole(array):
        zeros = (0,) * array.ndim
        return pl.BlockSpec(array.shape, lambda group, order_ref: zeros)

    def by_group(height):
        return pl.BlockSpec((height, lanes), lambda group, order_ref: (0, group))

    x_spec = pl.BlockSpec((rows, lanes), lambda group, order_ref: (0, 0))
    aux_spec = pl.BlockSpec(
        (rows, aux_lanes), lambda group, order_ref: (0, lanes // aux_lanes)
    )

    state_spec = pl.BlockSpec(
        (per_dev, heads, head_dim, state_width), lambda group, order_ref: (0, group, 0, 0)
    )
    step_lanes = select.shape[2] - 2 * state_width
    grid_spec = pltpu.PrefetchScalarGridSpec(
        num_scalar_prefetch=1,
        grid=(chunks,),
        in_specs=[
            *[x_spec] * chunks,
            *[aux_spec] * chunks,
            whole(select),
            whole(moves),
            whole(masks),
            by_group(hist_pad),
            whole(history_state),
            by_group(KCONV),
            whole(taps_state),
            pl.BlockSpec(memory_space=pltpu.SMEM),
            whole(steps),
            state_spec,
        ],
        out_specs=[
            by_group(rows),
            pl.BlockSpec((heads * head_dim, 2 * rows), lambda group, order_ref: (group, 0)),
            pl.BlockSpec((rows, state_width), lambda group, order_ref: (0, 0)),
            pl.BlockSpec((rows, step_lanes), lambda group, order_ref: (0, 0)),
            by_group(hist_pad),
            pl.BlockSpec((hist_pad, 2 * state_width), lambda group, order_ref: (0, 0)),
        ],
        scratch_shapes=[
            pltpu.VMEM((2 * state_width, 2 * rows), BF16),
            pltpu.VMEM((rows, rows), F32),
            pltpu.VMEM((chunks, rows, heads), F32),
            pltpu.VMEM((step_lanes, rows), F32),
            pltpu.VMEM((step_lanes, rows), F32),
            pltpu.VMEM((step_lanes, rows), F32),
        ],
    )
    return pl.pallas_call(
        lambda *refs: mixer_kernel(sizes, *refs),
        grid_spec=grid_spec,
        out_shape=(
            jax.ShapeDtypeStruct((rows, inner), BF16),
            jax.ShapeDtypeStruct((inner, 2 * rows), BF16),
            jax.ShapeDtypeStruct((rows, state_width), F32),
            jax.ShapeDtypeStruct((rows, step_lanes), F32),
            jax.ShapeDtypeStruct((hist_pad, inner), BF16),
            jax.ShapeDtypeStruct((hist_pad, 2 * state_width), BF16),
        ),
        compiler_params=pltpu.CompilerParams(vmem_limit_bytes=VMEM_LIMIT),
        cost_estimate=pl.CostEstimate(
            flops=64 * rows * rows * all_heads * head_dim,
            bytes_accessed=8 * state_pool.size,
            transcendentals=rows * rows * all_heads,
        ),
    )(
        order,
        *packed,
        *packed,
        select,
        moves,
        masks,
        history,
        history_state,
        taps,
        taps_state,
        skip_gain,
        steps,
        state_pool,
    )


def by_chunk(array, chunks, lanes):
    rows, width = array.shape
    parts = array.reshape(rows, chunks, width // chunks).transpose(1, 0, 2)
    return jnp.pad(parts, ((0, 0), (0, 0), (0, lanes - width // chunks)))


def swap(value, axis):
    return rotate(value, axis, 1)


def near_half(weight):
    me = lax.axis_index("near")
    keep = lax.dynamic_index_in_dim(weight, me, 0, keepdims=False)
    give = lax.dynamic_index_in_dim(weight, 1 - me, 0, keepdims=False)
    take = swap(give, "near")
    return jnp.concatenate([jnp.where(me == 0, keep, take), jnp.where(me == 0, take, keep)])


def tie(value, *others):
    return lax.optimization_barrier((value,) + others)[0]


def out_kernel(place_ref, rows_ref, *refs):
    weight_refs, out_ref = refs[:8], refs[8]
    for pair in range(4):
        weight = jnp.concatenate([weight_refs[2 * pair][...], weight_refs[2 * pair + 1][...]], axis=1)
        total = jnp.dot(rows_ref[...], weight, preferred_element_type=F32)
        for at in range(2):
            start = place_ref[(2 * pair + at) % 4] * LANES
            lanes = pl.ds(pl.multiple_of(start, LANES), LANES)
            columns = slice(at * LANES, (at + 1) * LANES)
            out_ref[pair // 2, :, lanes] = total[:, columns].astype(out_ref.dtype)


def project_out(rows, weights, place_of, dtype):
    whole = pl.BlockSpec(memory_space=pltpu.VMEM)
    return pl.pallas_call(
        out_kernel,
        in_specs=[pl.BlockSpec(memory_space=pltpu.SMEM)] + [whole] * 9,
        out_specs=whole,
        out_shape=jax.ShapeDtypeStruct((2, rows.shape[0], 4 * LANES), dtype),
        compiler_params=pltpu.CompilerParams(vmem_limit_bytes=24 * 1024 * 1024),
        cost_estimate=QUICK,
    )(place_of, rows, *weights)


def on_device(
    hidden_in,
    z_weight,
    x_weight,
    state_proj,
    step_weight,
    step_bias,
    decay_log,
    skip_gain,
    conv_inner,
    conv_state,
    norm_gain,
    out_weight,
    state_pool,
    conv_pool_inner,
    conv_pool_state,
    owner_dev,
    state_page,
    conv_page,
    accepted,
):
    groups = lax.axis_size(RING)
    fars, nears, sides, cores = (lax.axis_size(name) for name in RING)
    splits = lax.axis_size("mdl")
    paired = (fars, nears, sides, cores, splits) == (2, 2, 2, 2, 2)
    paired = paired and hidden_in.shape[1] == groups * LANES
    chunks = fars * nears if paired else nears
    this_dev = lax.axis_index(RING)
    near_at = lax.axis_index("near")
    me = lax.axis_index(SLABS) if paired else near_at
    part = lax.axis_index("mdl")
    per_dev, all_heads, head_dim, state_width = state_pool.shape
    rows, depth = hidden_in.shape
    draft = rows // per_dev
    inner = all_heads * head_dim
    slots = WINDOW * CAP
    chunk_width = inner // chunks
    lanes = chunk_width
    map_width = 2 * state_width // chunks
    heads = all_heads // chunks
    aux_lanes = round_up(map_width + heads, LANES)
    keep = KCONV - 1
    hist_rows = per_dev * keep
    hist_pad = round_up(hist_rows, 32)

    send_table, gather_table, conv_of, kept_count = route_tables(
        owner_dev, state_page, conv_page, accepted, groups, per_dev, this_dev
    )

    block = depth // groups
    columns = hidden_in.reshape(rows, fars, nears, sides, cores, block).transpose(0, 4, 3, 1, 2, 5)
    columns = columns.reshape(rows, splits, depth // splits)
    share = lax.dynamic_index_in_dim(columns, part, 1, keepdims=False)
    outgoing = one_hot_apply(send_table, share, (slots, draft, depth // splits))

    def prepare(after):
        conv_now, kept_now, pool_inner, pool_state, bias, rate = lax.optimization_barrier(
            (conv_of, kept_count, conv_pool_inner, conv_pool_state, step_bias, decay_log, after)
        )[:6]
        order = (jnp.arange(chunks, dtype=jnp.int32) - me) % chunks
        home_chunk = (jnp.arange(chunks, dtype=jnp.int32) + me) % chunks
        lane = jnp.arange(aux_lanes, dtype=jnp.int32)[None, :]
        step_lanes = round_up(all_heads, LANES)
        target = jnp.where(
            lane < map_width,
            home_chunk[:, None] * map_width + lane,
            jnp.where(
                lane < map_width + heads,
                2 * state_width + home_chunk[:, None] * heads + lane - map_width,
                -1,
            ),
        )
        select = (
            target[:, :, None] == jnp.arange(2 * state_width + step_lanes, dtype=jnp.int32)
        ).astype(BF16)
        tables = series_tables(conv_now, kept_now, per_dev, draft, hist_pad)
        pad_rows = ((0, hist_pad - hist_rows), (0, 0))
        history = jnp.pad(pool_inner.reshape(hist_rows, inner), pad_rows)
        history_state = jnp.pad(pool_state.reshape(hist_rows, 2 * state_width), pad_rows)
        pad_heads = ((0, 0), (0, step_lanes - all_heads))
        steps = jnp.pad(jnp.stack([bias, -jnp.exp(rate)]), pad_heads)
        return order, select, tables, history, history_state, steps

    def route(slots_out):
        return [
            rotate(slots_out[offset * CAP : (offset + 1) * CAP], RING, offset)
            for offset in range(WINDOW)
        ]

    packed_weight = jnp.concatenate(
        [
            by_chunk(x_weight, chunks, lanes),
            by_chunk(state_proj, chunks, map_width),
            by_chunk(step_weight, chunks, aux_lanes - map_width),
            by_chunk(z_weight, chunks, lanes),
        ],
        axis=2,
    )
    split = lanes + aux_lanes
    width = split + lanes
    far, side, core = (lax.axis_index(name) for name in ("far", "side", "core"))
    if paired:
        incoming = route(outgoing)
        packed_weight, early = lax.optimization_barrier((packed_weight, incoming[: WINDOW - 2]))
        pieces = [
            rotate(
                lax.dynamic_index_in_dim(packed_weight, (me + step) % chunks, 0, keepdims=False),
                SLABS,
                step,
            )
            for step in range(chunks)
        ]
        side_own = swap(pieces[0], "side")
        extras = prepare(early)
        incoming, pieces, side_own, extras = lax.optimization_barrier(
            (early + incoming[WINDOW - 2 :], pieces, side_own, extras)
        )
        owned = one_hot_apply(gather_table, jnp.concatenate(incoming), (rows, depth // splits))
        owned, pieces = lax.optimization_barrier((owned, pieces))
        rows_of = [rotate(owned, SLABS, step) for step in range(chunks)]
        slabs = [(me - step) % chunks for step in range(chunks)]
        across = swap(jnp.stack(pieces[1:]), "side")
        held = place(pieces, slabs)
        rows_of, across, held = lax.optimization_barrier((rows_of, across, held))
        out_far, out_side = swap(out_weight, "far"), swap(out_weight, "side")
        across = place([side_own] + [across[at] for at in range(chunks - 1)], slabs)
        held, across = held.reshape(-1, width), across.reshape(-1, width)
        weights = jnp.concatenate([held, across, swap(held, "core"), swap(across, "core")])
        early_own = jnp.concatenate(rows_of[1:3])
        late_own = jnp.concatenate([rows_of[3], rows_of[0]])
        early_peer = swap(early_own, "mdl")
        early_own, early_peer, late_own, weights, out_side = lax.optimization_barrier(
            (early_own, early_peer, late_own, weights, out_side)
        )

        def project(own, peer):
            low = jnp.where(part == core, own, peer)
            high = jnp.where(part == core, peer, own)
            quarter = depth // 4
            lhs = [
                lax.dynamic_slice_in_dim(value, at_side * quarter, quarter, 1)
                for value in (low, high)
                for at_side in (side, 1 - side)
            ]
            total = jnp.dot(jnp.concatenate(lhs, axis=1), weights, preferred_element_type=F32)
            return total.astype(BF16)

        late_peer = swap(late_own, "mdl")
        early = project(early_own, early_peer)
        packed_1 = rotate(early[:rows, :split], SLABS, -1)
        packed_2 = rotate(early[rows:, :split], SLABS, -2)
        late = project(late_own, late_peer)
        packed_3 = rotate(late[:rows, :split], SLABS, -3)
        out_across = swap(tie(out_far, late), "side")
        gate = [late[rows:, split:], early[:rows, split:], early[rows:, split:], late[:rows, split:]]
        packed = [late[rows:, :split], packed_1, packed_2, packed_3]
        gate, packed = lax.optimization_barrier((gate, packed))
        gate = [rotate(value, SLABS, -step) for step, value in enumerate(gate)]
        out_columns = []
        for column in (out_weight, out_side, out_far, out_across):
            out_columns += [column, swap(column, "core")]
    else:
        incoming = route(outgoing)
        extras = prepare(outgoing)
        owned = one_hot_apply(gather_table, jnp.concatenate(incoming), (rows, depth // splits))
        owned = lax.all_gather(owned, "mdl", axis=1, tiled=True)
        owned = jnp.concatenate([owned, swap(owned, "near")])
        weight = near_half(packed_weight)
        for name in ("far", "side", "core"):
            weight = lax.all_gather(weight, name, axis=0, tiled=True)
        total = jnp.dot(owned, weight, preferred_element_type=F32).astype(BF16)
        total = [total[:rows], swap(total[rows:], "near")]
        packed = [value[:, :split] for value in total]
        gate = [value[:, split:] for value in total]
        out_columns = lax.all_gather(out_weight, RING, axis=1, tiled=True)

    order, select, tables, history, history_state, steps = extras
    y_rows, picked, b_rows, ends, conv_rows, conv_state_rows = mix_requests(
        packed,
        order,
        select,
        tables,
        history,
        history_state,
        conv_inner,
        conv_state,
        skip_gain,
        steps,
        state_pool,
    )

    gate_here = []
    for chunk in range(chunks):
        value = gate[0]
        for step in range(1, chunks):
            value = jnp.where(me == (chunk - step) % chunks, gate[step], value)
        gate_here.append(value)
    gate_here = jnp.concatenate(gate_here, axis=1).astype(F32)
    gated = y_rows.astype(F32) * (gate_here / (1.0 + jnp.exp(-gate_here)))
    squares = jnp.sum(gated * gated, axis=1)
    scaled = (gated * norm_gain).astype(BF16)
    new_states = update_states(picked, tie(b_rows, scaled), ends, state_pool)
    wide = depth // splits
    total_inner = inner * splits
    if paired:
        squares = squares + swap(squares, "mdl")
        scale = lax.rsqrt(squares / total_inner + EPSILON)
        columns_at = jnp.stack(
            [2 * at_side + at_core for at_side in (side, 1 - side) for at_core in (core, 1 - core)]
        )
        terms = project_out(scaled, out_columns, columns_at, F32)
        given = project_out(
            tie(swap(scaled, "near"), new_states, terms), out_columns, columns_at, BF16
        )
        here = far == part
        mine = jnp.where(here, terms[0], terms[1])
        other = jnp.where(here, terms[1], terms[0]).astype(BF16)
        peer_mine = jnp.where(here, given[0], given[1])
        peer_other = jnp.where(here, given[1], given[0])
        over_y = swap(other, "mdl")
        over_near = swap(peer_mine, "near")
        over_both = lax.ppermute(peer_other, ("near", "mdl"), [(0, 3), (1, 2), (2, 1), (3, 0)])
        here = (mine + over_y.astype(F32)) * scale[:, None]
        there = (over_near.astype(F32) + over_both.astype(F32)) * scale[:, None]
        here, there = here.astype(BF16), there.astype(BF16)
        mixed_rows = jnp.concatenate(
            [jnp.where(near_at == 0, here, there), jnp.where(near_at == 0, there, here)], axis=1
        )
    else:
        terms = jnp.dot(scaled, out_columns, preferred_element_type=F32)
        squares = lax.psum(squares, "mdl")
        total = lax.psum_scatter(terms, "mdl", scatter_dimension=1, tiled=True)
        scale = lax.rsqrt(squares / total_inner + EPSILON)
        mixed_rows = (total * scale[:, None]).astype(BF16)

    returning = one_hot_apply(
        gather_table.T, mixed_rows.reshape(per_dev, draft, wide), (slots, draft, wide)
    )
    arrived = jnp.concatenate(
        [
            rotate(returning[offset * CAP : (offset + 1) * CAP], RING, -offset)
            for offset in range(WINDOW)
        ],
        axis=0,
    )
    mixed = one_hot_apply(send_table.T, arrived, (rows, wide))
    return (
        mixed,
        new_states,
        conv_rows[:hist_rows].reshape(per_dev, keep, inner),
        conv_state_rows[:hist_rows].reshape(per_dev, keep, 2 * state_width),
    )


def solution(mesh):
    sizes = factor(mesh.shape["req"])
    split_mesh = Mesh(mesh.devices.reshape(*sizes, mesh.shape["mdl"]), RING + ("mdl",))
    return jax.shard_map(
        on_device,
        mesh=split_mesh,
        in_specs=(
            P(RING, None),
            P(RING, "mdl"),
            P(RING, "mdl"),
            P(RING, None),
            P(RING, "mdl"),
            P("mdl"),
            P("mdl"),
            P("mdl"),
            P(None, "mdl"),
            P(),
            P("mdl"),
            P("mdl", RING),
            P(RING, "mdl", None, None),
            P(RING, None, "mdl"),
            P(RING, None, None),
            P(),
            P(),
            P(),
            P(),
        ),
        out_specs=(
            P(RING, "mdl"),
            P(RING, "mdl", None, None),
            P(RING, None, "mdl"),
            P(RING, None, None),
        ),
        check_vma=False,
    )
```
